32 devices in a mesh: nodes: 8 (over y, x, core), feat: 4 (over z).
Axes of the slice: x: 2, y: 2, z: 4, core: 2. Of those that a mesh axis runs over, the one named last changes fastest.
Arguments:
- feats: bfloat16 [65536, 128], P('nodes', 'feat'), may hold values from -6 to 6
- tiles: bfloat16 [8, 8, 32, 128, 128], P('nodes'), may hold values from -0.375 to 0.375
- dst_block: int32 [8, 8, 32], P('nodes'), may hold values from 0 to 63
- src_block: int32 [8, 8, 32], P('nodes'), may hold values from 0 to 63
- tile_counts: int32 [8, 8], P('nodes'), may hold values from 1 to 32, as said below
- norm: float32 [65536], P('nodes'), may hold values from 0.3 to 3
- weight: bfloat16 [128, 256], P('feat'), may hold values from -0.5 to 0.5
- bias: float32 [256], P('feat'), may hold values from -3 to 3
- cotangent: bfloat16 [65536, 256], P('nodes', 'feat'), may hold values from -6 to 6
Outputs:
- hidden: bfloat16 [65536, 256], P('nodes', 'feat')
- grad_weight: float32 [128, 256], P('feat')
- grad_bias: float32 [256], P('feat')
- grad_feats: float32 [65536, 128], P('nodes', 'feat')
The draws below stay inside these ranges and needn't reach their ends.
Inputs may be any that keep to these rules, and one draw needn't show every extreme that they name: Slots at or past tile_counts[o, p] hold no tile; one source slab has 32 tiles from every owner slab in every draw.
All inputs are finite; a program needn't handle non-finite values.
Results may differ from the reference program's by a relative error of at most 0.0075.
Values may be sent and summed in bfloat16 or wider, within the bound.
A program may use at most 128 MiB of HBM per device.

```python
import math
import jax
import jax.numpy as jnp
from jax import lax

FIN = 128
HID = 256
TILE = 128
BLK = 64
CAP = 32
SLABS = 8
NODES = 65536


def draw_tile_counts(key, part):
    level_key, drawn_key, column_key = jax.random.split(key, 3)
    level = jax.random.randint(level_key, (SLABS, 1), 0, 4)
    drawn = jax.random.randint(drawn_key, (SLABS, SLABS), 1, CAP + 1)
    counts = jnp.clip(drawn - (3 - level) * CAP // 8, 1, CAP)
    column = jax.random.randint(column_key, (), 0, SLABS)
    filled = jnp.where(jnp.arange(SLABS)[None, :] == column, CAP, counts)
    return filled.astype(jnp.int32)


def touch_ends(values, own_key, least, high):
    longest = values.shape.index(max(values.shape))
    spots = []
    for shift in (0, 1):
        where = [jax.random.randint(jax.random.fold_in(own_key, axis), (), 0, length) for axis, length in enumerate(values.shape)]
        where[longest] = (where[longest] + shift) % values.shape[longest]
        spots.append(tuple(where))
    return values.at[spots[0]].set(least).at[spots[1]].set(high)


def steps_of(key, dims, cuts, least, top_value):
    gain = 1.0
    for axis_at, blocks in cuts:
        steps = jax.random.uniform(jax.random.fold_in(jax.random.fold_in(key, 6), axis_at), (blocks,), jnp.float32, least / len(cuts), top_value / len(cuts))
        gain = gain * jnp.repeat(jnp.exp(steps), dims[axis_at] // blocks).reshape((-1,) + (1,) * (len(dims) - 1 - axis_at))
    return gain


def scatter_about(key, dims, scale, bound, pieces=(), kind=jnp.bfloat16):
    values = scale * jax.random.normal(key, dims, jnp.float32)
    if pieces:
        values = values * steps_of(key, dims, pieces, -0.22, 0.18)
    return jnp.clip(values, -bound, bound).astype(kind)


def setup_inputs(seed: int = 0) -> dict:
    splits = jax.random.split(jax.random.key(seed), 10)
    feats = scatter_about(splits[0], (NODES, FIN), 1.0, 6.0, ((0, 8), (1, 4)))
    tiles = scatter_about(splits[1], (SLABS, SLABS, CAP, TILE, TILE), (TILE * SLABS * CAP // (2 * BLK)) ** -0.5, 0.375, ((0, 8),))
    dst_block = touch_ends(jax.random.randint(splits[2], (SLABS, SLABS, CAP), 0, BLK), jax.random.fold_in(splits[2], 1), 0, BLK - 1).astype(jnp.int32)
    src_block = touch_ends(jax.random.randint(splits[3], (SLABS, SLABS, CAP), 0, BLK), jax.random.fold_in(splits[3], 1), 0, BLK - 1).astype(jnp.int32)
    tile_counts = draw_tile_counts(jax.random.fold_in(splits[9], 71), 0)
    norm = jnp.clip(jnp.exp(math.log(3.0) - 2.3025851 * jax.random.uniform(splits[5], (NODES,), jnp.float32) ** steps_of(splits[5], (NODES,), ((0, 8),), -0.2, 0.2)), 0.3, 3.0)
    weight = scatter_about(splits[6], (FIN, HID), FIN ** -0.5, 0.5, ((0, 4),))
    bias = scatter_about(splits[7], (HID,), 0.5, 3.0, ((0, 4),), jnp.float32)
    cotangent = scatter_about(splits[8], (NODES, HID), 1.0, 6.0, ((0, 8), (1, 4)))
    return {"feats": feats, "tiles": tiles, "dst_block": dst_block, "src_block": src_block, "tile_counts": tile_counts, "norm": norm, "weight": weight, "bias": bias, "cotangent": cotangent}


def reference(feats, tiles, dst_block, src_block, tile_counts, norm, weight, bias, cotangent):
    highest = lax.Precision.HIGHEST
    scaled = (norm[:, None] * feats.astype(jnp.float32)).astype(jnp.bfloat16)
    scaled_blocks = scaled.reshape(SLABS, BLK, TILE, FIN)
    slot_ids = jnp.arange(CAP, dtype=jnp.int32)
    block_ids = jnp.arange(BLK, dtype=jnp.int32)
    peer_ids = jnp.arange(SLABS, dtype=jnp.int32)

    def forward_owner(owner):
        tile_set = tiles[owner].astype(jnp.float32)
        picked = scaled_blocks[peer_ids[:, None], src_block[owner]].astype(jnp.float32)
        product = jnp.einsum("pcij,pcjf->pcif", tile_set, picked, precision=highest)
        usable = (slot_ids[None, :] < tile_counts[owner][:, None]).astype(jnp.float32)
        placing = (dst_block[owner][..., None] == block_ids).astype(jnp.float32) * usable[..., None]
        return jnp.einsum("pcb,pcif->bif", placing, product, precision=highest)

    summed = lax.map(forward_owner, peer_ids)
    aggregated = (norm[:, None] * summed.reshape(NODES, FIN)).astype(jnp.bfloat16)
    pre = jnp.dot(aggregated, weight, preferred_element_type=jnp.float32) + bias
    hidden = jax.nn.silu(pre).astype(jnp.bfloat16)
    sigma = jax.nn.sigmoid(pre)
    grad_pre = (cotangent.astype(jnp.float32) * sigma * (1.0 + pre * (1.0 - sigma))).astype(jnp.bfloat16)
    scale = NODES ** -0.5
    grad_weight = jnp.dot(aggregated.T, grad_pre, preferred_element_type=jnp.float32) * scale
    grad_bias = jnp.sum(grad_pre.astype(jnp.float32), axis=0) * scale
    back_scaled = (norm[:, None] * jnp.dot(grad_pre, weight.T, preferred_element_type=jnp.float32)).astype(jnp.bfloat16)
    back_blocks = back_scaled.reshape(SLABS, BLK, TILE, FIN)

    def backward_owner(carry, owner):
        tile_set = tiles[owner].astype(jnp.float32)
        picked = back_blocks[owner][dst_block[owner]].astype(jnp.float32)
        usable = (slot_ids[None, :] < tile_counts[owner][:, None]).astype(jnp.float32)
        partial_back = jnp.einsum("pcij,pcif->pcjf", tile_set, picked, precision=highest) * usable[:, :, None, None]
        placing = (src_block[owner][..., None] == block_ids).astype(jnp.float32)
        return carry + jnp.einsum("pcb,pcjf->pbjf", placing, partial_back, precision=highest), None

    start_total = jnp.zeros((SLABS, BLK, TILE, FIN), jnp.float32)
    returned, unused = lax.scan(backward_owner, start_total, peer_ids)
    grad_feats = norm[:, None] * returned.reshape(NODES, FIN)
    return hidden, grad_weight, grad_bias, grad_feats
```

```python
import functools

import jax
import jax.numpy as jnp
from jax import lax
from jax.experimental import pallas as pl
from jax.experimental.pallas import tpu as pltpu
from jax.sharding import PartitionSpec as P

GROUP = 4
NT = (((1,), (1,)), ((), ()))
NN = (((1,), (0,)), ((), ()))


def tile_products(n, tiles_ref, x_of, reads, writes, acc, dims):
    size = tiles_ref.shape[-1]
    slots = tiles_ref.shape[2]
    width = GROUP if slots % GROUP == 0 else 1

    def group(g, carry):
        products = []
        for k in range(width):
            slot = g * width + k
            x = x_of(pl.ds(pl.multiple_of(reads(slot) * size, size), size))
            x = jnp.where(slot < n, x, jnp.zeros_like(x))
            products.append(
                lax.dot_general(x, tiles_ref[0, 0, slot], dims, preferred_element_type=jnp.float32)
            )
        for k in range(width):
            place = writes(g * width + k)
            acc[place] = acc[place] + products[k]
        return carry

    lax.fori_loop(0, (n + width - 1) // width, group, 0)


def forward_kernel(counts, src, dst, tiles_ref, x_ref, norm_ref, out_ref, acc):
    peer = pl.program_id(0)
    size = tiles_ref.shape[-1]

    @pl.when(peer == 0)
    def _():
        acc[...] = jnp.zeros_like(acc)

    tile_products(
        counts[0, peer],
        tiles_ref,
        lambda cut: x_ref[0, :, cut],
        lambda slot: src[peer, slot],
        lambda slot: dst[peer, slot],
        acc,
        NT,
    )

    @pl.when(peer == pl.num_programs(0) - 1)
    def _():
        for b in range(acc.shape[0]):
            cut = slice(b * size, (b + 1) * size)
            out_ref[:, cut] = (norm_ref[:, cut] * acc[b]).astype(out_ref.dtype)


def backward_kernel(counts, src, dst, tiles_ref, x_ref, out_ref, acc):
    peer = pl.program_id(0)
    size = tiles_ref.shape[-1]
    acc[...] = jnp.zeros_like(acc)
    tile_products(
        counts[0, peer],
        tiles_ref,
        lambda cut: x_ref[:, cut],
        lambda slot: dst[peer, slot],
        lambda slot: src[peer, slot],
        acc,
        NN,
    )
    for b in range(acc.shape[0]):
        out_ref[0, :, b * size : (b + 1) * size] = acc[b].astype(out_ref.dtype)


def forward_tiles(counts, src, dst, tiles, x, norm):
    _, slabs, slots, size, _ = tiles.shape
    feat, rows = x.shape[1:]
    return pl.pallas_call(
        forward_kernel,
        grid_spec=pltpu.PrefetchScalarGridSpec(
            num_scalar_prefetch=3,
            grid=(slabs,),
            in_specs=[
                pl.BlockSpec((1, 1, slots, size, size), lambda p, *_: (0, p, 0, 0, 0)),
                pl.BlockSpec((1, feat, rows), lambda p, *_: (p, 0, 0)),
                pl.BlockSpec((1, rows), lambda p, *_: (0, 0)),
            ],
            out_specs=pl.BlockSpec((feat, rows), lambda p, *_: (0, 0)),
            scratch_shapes=[pltpu.VMEM((rows // size, feat, size), jnp.float32)],
        ),
        out_shape=jax.ShapeDtypeStruct((feat, rows), jnp.bfloat16),
        compiler_params=pltpu.CompilerParams(vmem_limit_bytes=32 << 20),
        name="forward_tiles",
    )(counts, src, dst, tiles, x, norm)


def backward_tiles(counts, src, dst, tiles, x):
    _, slabs, slots, size, _ = tiles.shape
    feat, rows = x.shape
    return pl.pallas_call(
        backward_kernel,
        grid_spec=pltpu.PrefetchScalarGridSpec(
            num_scalar_prefetch=3,
            grid=(slabs,),
            in_specs=[
                pl.BlockSpec((1, 1, slots, size, size), lambda p, *_: (0, p, 0, 0, 0)),
                pl.BlockSpec((feat, rows), lambda p, *_: (0, 0)),
            ],
            out_specs=pl.BlockSpec((1, feat, rows), lambda p, *_: (p, 0, 0)),
            scratch_shapes=[pltpu.VMEM((rows // size, feat, size), jnp.float32)],
        ),
        out_shape=jax.ShapeDtypeStruct((slabs, feat, rows), jnp.bfloat16),
        compiler_params=pltpu.CompilerParams(vmem_limit_bytes=32 << 20),
        name="backward_tiles",
    )(counts, src, dst, tiles, x)


def on_device(feats, tiles, dst_block, src_block, tile_counts, norm, weight, bias, cotangent):
    rows, feat_local = feats.shape
    hid_local = cotangent.shape[1]
    nodes, parts = lax.axis_size("nodes"), lax.axis_size("feat")
    quarter = rows // parts
    norm_row = norm[None, :]
    counts, src, dst = tile_counts, src_block[0], dst_block[0]
    scaled = (norm_row * feats.T.astype(jnp.float32)).astype(jnp.bfloat16)
    cot = lax.all_to_all(cotangent.T, "feat", 1, 0, tiled=True)
    full_weight = lax.all_gather(weight, "feat", axis=0, tiled=True)
    full_bias = lax.all_gather(bias, "feat", axis=0, tiled=True)
    shards = lax.all_gather(scaled, "nodes", axis=0)
    aggregated = forward_tiles(counts, src, dst, tiles, shards, norm_row)
    agg = lax.all_to_all(aggregated, "feat", 1, 0, tiled=True)
    pre = (
        lax.dot_general(full_weight, agg, (((0,), (0,)), ((), ())), preferred_element_type=jnp.float32)
        + full_bias[:, None]
    )
    sigma = jax.nn.sigmoid(pre)
    hidden = (pre * sigma).astype(jnp.bfloat16)
    grad_pre = (cot.astype(jnp.float32) * (sigma * (1.0 + pre * (1.0 - sigma)))).astype(jnp.bfloat16)
    norm_part = lax.dynamic_slice_in_dim(norm_row, lax.axis_index("feat") * quarter, quarter, 1)
    back = (
        norm_part * lax.dot_general(full_weight, grad_pre, NN, preferred_element_type=jnp.float32)
    ).astype(jnp.bfloat16)
    back = lax.all_to_all(back, "feat", 0, 1, tiled=True)
    partial = backward_tiles(counts, src, dst, tiles, back)
    hidden = lax.all_to_all(hidden, "feat", 0, 1, tiled=True)
    scale = (rows * nodes) ** (-0.5)
    weight_part = lax.dot_general(agg, grad_pre, NT, preferred_element_type=jnp.float32)
    bias_part = jnp.sum(grad_pre, axis=1, dtype=jnp.float32)
    weight_sum, bias_sum = lax.psum((weight_part, bias_part), ("nodes", "feat"))
    me = lax.axis_index("feat")
    grad_weight = lax.dynamic_slice_in_dim(weight_sum, me * feat_local, feat_local, 0) * scale
    grad_bias = lax.dynamic_slice_in_dim(bias_sum, me * hid_local, hid_local, 0) * scale
    returned = lax.psum_scatter(partial, "nodes", scatter_dimension=0, tiled=False)
    grad_feats = norm_row * returned.astype(jnp.float32)
    return (hidden.T, grad_weight, grad_bias, grad_feats.T)


def solution(mesh):
    return jax.shard_map(
        on_device,
        mesh=mesh,
        in_specs=(
            P("nodes", "feat"),
            P("nodes", None, None, None, None),
            P("nodes", None, None),
            P("nodes", None, None),
            P("nodes", None),
            P("nodes"),
            P("feat", None),
            P("feat"),
            P("nodes", "feat"),
        ),
        out_specs=(P("nodes", "feat"), P("feat", None), P("feat"), P("nodes", "feat")),
        check_vma=False,
    )
```

```python
import functools

import jax
import jax.numpy as jnp
from jax import lax
from jax.experimental import pallas as pl
from jax.experimental.pallas import tpu as pltpu
from jax.sharding import PartitionSpec as P

GROUP = 4
NT = (((1,), (1,)), ((), ()))
NN = (((1,), (0,)), ((), ()))


def tile_products(n, tiles_ref, x_of, reads, writes, acc, dims):
    size = tiles_ref.shape[-1]
    slots = tiles_ref.shape[2]
    width = GROUP if slots % GROUP == 0 else 1

    def group(g, carry):
        products = []
        for k in range(width):
            slot = g * width + k
            x = x_of(pl.ds(pl.multiple_of(reads(slot) * size, size), size))
            x = jnp.where(slot < n, x, jnp.zeros_like(x))
            products.append(
                lax.dot_general(x, tiles_ref[0, 0, slot], dims, preferred_element_type=jnp.float32)
            )
        for k in range(width):
            place = writes(g * width + k)
            acc[place] = acc[place] + products[k]
        return carry

    lax.fori_loop(0, (n + width - 1) // width, group, 0)


def forward_kernel(counts, src, dst, tiles_ref, x_ref, norm_ref, out_ref, acc):
    peer = pl.program_id(0)
    size = tiles_ref.shape[-1]

    @pl.when(peer == 0)
    def _():
        acc[...] = jnp.zeros_like(acc)

    tile_products(
        counts[0, peer],
        tiles_ref,
        lambda cut: x_ref[0, :, cut],
        lambda slot: src[peer, slot],
        lambda slot: dst[peer, slot],
        acc,
        NT,
    )

    @pl.when(peer == pl.num_programs(0) - 1)
    def _():
        for b in range(acc.shape[0]):
            cut = slice(b * size, (b + 1) * size)
            out_ref[:, cut] = (norm_ref[:, cut] * acc[b]).astype(out_ref.dtype)


def backward_kernel(counts, src, dst, tiles_ref, x_ref, out_ref, acc):
    peer = pl.program_id(0)
    size = tiles_ref.shape[-1]
    acc[...] = jnp.zeros_like(acc)
    tile_products(
        counts[0, peer],
        tiles_ref,
        lambda cut: x_ref[:, cut],
        lambda slot: dst[peer, slot],
        lambda slot: src[peer, slot],
        acc,
        NN,
    )
    for b in range(acc.shape[0]):
        out_ref[0, :, b * size : (b + 1) * size] = acc[b].astype(out_ref.dtype)


def forward_tiles(counts, src, dst, tiles, x, norm):
    _, slabs, slots, size, _ = tiles.shape
    feat, rows = x.shape[1:]
    return pl.pallas_call(
        forward_kernel,
        grid_spec=pltpu.PrefetchScalarGridSpec(
            num_scalar_prefetch=3,
            grid=(slabs,),
            in_specs=[
                pl.BlockSpec((1, 1, slots, size, size), lambda p, *_: (0, p, 0, 0, 0)),
                pl.BlockSpec((1, feat, rows), lambda p, *_: (p, 0, 0)),
                pl.BlockSpec((1, rows), lambda p, *_: (0, 0)),
            ],
            out_specs=pl.BlockSpec((feat, rows), lambda p, *_: (0, 0)),
            scratch_shapes=[pltpu.VMEM((rows // size, feat, size), jnp.float32)],
        ),
        out_shape=jax.ShapeDtypeStruct((feat, rows), jnp.bfloat16),
        compiler_params=pltpu.CompilerParams(vmem_limit_bytes=32 << 20),
        name="forward_tiles",
    )(counts, src, dst, tiles, x, norm)


def backward_tiles(counts, src, dst, tiles, x):
    _, slabs, slots, size, _ = tiles.shape
    feat, rows = x.shape
    return pl.pallas_call(
        backward_kernel,
        grid_spec=pltpu.PrefetchScalarGridSpec(
            num_scalar_prefetch=3,
            grid=(slabs,),
            in_specs=[
                pl.BlockSpec((1, 1, slots, size, size), lambda p, *_: (0, p, 0, 0, 0)),
                pl.BlockSpec((feat, rows), lambda p, *_: (0, 0)),
            ],
            out_specs=pl.BlockSpec((1, feat, rows), lambda p, *_: (p, 0, 0)),
            scratch_shapes=[pltpu.VMEM((rows // size, feat, size), jnp.float32)],
        ),
        out_shape=jax.ShapeDtypeStruct((slabs, feat, rows), jnp.bfloat16),
        compiler_params=pltpu.CompilerParams(vmem_limit_bytes=32 << 20),
        name="backward_tiles",
    )(counts, src, dst, tiles, x)


def remote(src, dst, send, recv, target):
    return pltpu.make_async_remote_copy(
        src_ref=src,
        dst_ref=dst,
        send_sem=send,
        recv_sem=recv,
        device_id=target,
        device_id_type=pl.DeviceIdType.MESH,
    )


def greet(targets):
    barrier = pltpu.get_barrier_semaphore()
    for target in targets:
        pl.semaphore_signal(
            barrier, inc=1, device_id=target, device_id_type=pl.DeviceIdType.MESH
        )
    pl.semaphore_wait(barrier, len(targets))


def gather_kernel(
    nodes, parts, pieces,
    feats_ref, norm_ref, weight_ref, bias_ref,
    out_ref, weight_out, bias_out,
    scaled, own_sem, send_sem, recv_sem, pass_send, pass_recv, small_send, small_recv,
):
    node, part = lax.axis_index("nodes"), lax.axis_index("feat")
    chips = nodes // 2
    chip, core = node // 2, node % 2
    sibling = {"nodes": chip * 2 + 1 - core}
    width = scaled.shape[1] // pieces
    cuts = [pl.ds(k * width, width) for k in range(pieces)]
    chip_at = lambda d: (chip + d) % chips
    node_at = lambda d: {"nodes": chip_at(d) * 2 + core}
    part_at = lambda d: {"feat": (part + d) % parts}
    greet([sibling] + [node_at(d) for d in range(1, chips)] + [part_at(d) for d in range(1, parts)])

    started = []
    for d in range(1, parts):
        for k, (src, dst) in enumerate(((weight_ref, weight_out), (bias_ref, bias_out))):
            copy = remote(src, dst.at[part], small_send.at[d, k], small_recv.at[d, k], part_at(d))
            copy.start()
            started.append(copy)
    weight_out[part] = weight_ref[...]
    bias_out[part] = bias_ref[...]

    direct = {}
    own = []
    passed = []
    for k, cut in enumerate(cuts):
        scaled[:, cut] = (norm_ref[:, cut] * feats_ref[:, cut].astype(jnp.float32)).astype(scaled.dtype)
        place = out_ref.at[node, :, cut]
        for d in range(1, chips):
            copy = remote(scaled.at[:, cut], place, send_sem.at[d, k], recv_sem.at[d, k], node_at(d))
            copy.start()
            direct[d, k] = copy
        copy = remote(scaled.at[:, cut], place, pass_send.at[0, k], pass_recv.at[0, k], sibling)
        copy.start()
        passed.append(copy)
        copy = pltpu.make_async_copy(scaled.at[:, cut], place, own_sem.at[k])
        copy.start()
        own.append(copy)
    for k, cut in enumerate(cuts):
        for d in range(1, chips):
            direct[d, k].wait_recv()
            place = out_ref.at[chip_at(chips - d) * 2 + core, :, cut]
            copy = remote(place, place, pass_send.at[d, k], pass_recv.at[d, k], sibling)
            copy.start()
            passed.append(copy)
    for copy in own:
        copy.wait()
    for copy in started + passed:
        copy.wait()
    for copy in direct.values():
        copy.wait_send()


def gather_nodes(feats, norm, weight, bias, nodes, parts, pieces=4):
    feat, rows = feats.shape
    dma = pltpu.SemaphoreType.DMA
    chips = nodes // 2
    vmem = pl.BlockSpec(memory_space=pltpu.VMEM)
    return pl.pallas_call(
        functools.partial(gather_kernel, nodes, parts, pieces),
        out_shape=(
            jax.ShapeDtypeStruct((nodes, feat, rows), jnp.bfloat16),
            jax.ShapeDtypeStruct((parts,) + weight.shape, weight.dtype),
            jax.ShapeDtypeStruct((parts,) + bias.shape, bias.dtype),
        ),
        in_specs=[vmem] * 4,
        out_specs=(pl.BlockSpec(memory_space=pl.ANY), vmem, vmem),
        scratch_shapes=[
            pltpu.VMEM((feat, rows), jnp.bfloat16),
            dma((pieces,)),
            dma((chips, pieces)),
            dma((chips, pieces)),
            dma((chips, pieces)),
            dma((chips, pieces)),
            dma((parts, 2)),
            dma((parts, 2)),
        ],
        compiler_params=pltpu.CompilerParams(
            collective_id=0, has_side_effects=True, vmem_limit_bytes=32 << 20
        ),
        name="gather_nodes",
    )(feats, norm, weight, bias)


def scatter_kernel(
    nodes, parts, scale,
    partial_ref, norm_ref, sums_ref,
    out_ref, sums_out,
    sibling_buf, stage, arrived, small_part, small_stage, small_node,
    pass_send, pass_recv, send_sem, recv_sem, ps_send, ps_recv, ns_send, ns_recv,
):
    node, part = lax.axis_index("nodes"), lax.axis_index("feat")
    chips = nodes // 2
    chip, core = node // 2, node % 2
    rows = partial_ref.shape[2]
    step = min(rows, 1024)
    other = chip * 2 + 1 - core
    chip_at = lambda d: (chip + d) % chips
    node_at = lambda d: {"nodes": chip_at(d) * 2 + core}
    any_node = lambda d: {"nodes": (node + d) % nodes}
    part_at = lambda d: {"feat": (part + d) % parts}
    greet([any_node(d) for d in range(1, nodes)] + [part_at(d) for d in range(1, parts)])

    part_copies = []
    for d in range(1, parts):
        copy = remote(
            sums_ref.at[(part + d) % parts], small_part.at[d], ps_send.at[d], ps_recv.at[d], part_at(d)
        )
        copy.start()
        part_copies.append(copy)
    order = list(range(1, chips)) + [0]
    passes = {}
    for d in order:
        copy = remote(
            partial_ref.at[chip_at(d) * 2 + 1 - core],
            sibling_buf.at[d],
            pass_send.at[d],
            pass_recv.at[d],
            {"nodes": other},
        )
        copy.start()
        passes[d] = copy

    for copy in part_copies:
        copy.wait_recv()
    small_stage[...] = sums_ref[part]
    for d in range(1, parts):
        small_stage[...] += small_part[d]
    node_copies = []
    for d in range(1, nodes):
        copy = remote(small_stage, small_node.at[node], ns_send.at[d], ns_recv.at[d], any_node(d))
        copy.start()
        node_copies.append(copy)

    directs = []
    for d in order:
        passes[d].wait_recv()
        mine = chip_at(d) * 2 + core

        @pl.loop(0, rows // step)
        def _(i):
            cut = pl.ds(pl.multiple_of(i * step, step), step)
            total = partial_ref[mine, :, cut].astype(jnp.float32) + sibling_buf[d, :, cut].astype(jnp.float32)
            if d == 0:
                out_ref[:, cut] = total
            else:
                stage[d, :, cut] = total.astype(stage.dtype)

        if d:
            copy = remote(stage.at[d], arrived.at[d], send_sem.at[d], recv_sem.at[d], node_at(d))
            copy.start()
            directs.append(copy)
    for copy in node_copies:
        copy.wait_recv()
    small_node[node] = small_stage[...]
    total = small_node[0]
    for d in range(1, nodes):
        total = total + small_node[d]
    sums_out[...] = total * scale
    for copy in directs:
        copy.wait_recv()

    @pl.loop(0, rows // step)
    def _(i):
        cut = pl.ds(pl.multiple_of(i * step, step), step)
        total = out_ref[:, cut]
        for d in range(1, chips):
            total = total + arrived[d, :, cut].astype(jnp.float32)
        out_ref[:, cut] = norm_ref[:, cut] * total

    for copy in part_copies + node_copies + list(passes.values()) + directs:
        copy.wait_send()


def scatter_nodes(partial, norm, sums, parts, scale):
    nodes, feat, rows = partial.shape
    dma = pltpu.SemaphoreType.DMA
    chips = nodes // 2
    vmem = pl.BlockSpec(memory_space=pltpu.VMEM)
    big = pltpu.VMEM((chips, feat, rows), jnp.bfloat16)
    small = sums.shape[1:]
    return pl.pallas_call(
        functools.partial(scatter_kernel, nodes, parts, scale),
        out_shape=(
            jax.ShapeDtypeStruct((feat, rows), jnp.float32),
            jax.ShapeDtypeStruct(small, jnp.float32),
        ),
        in_specs=[vmem] * 3,
        out_specs=(vmem, vmem),
        scratch_shapes=[
            big, big, big,
            pltpu.VMEM((parts,) + small, jnp.float32),
            pltpu.VMEM(small, jnp.float32),
            pltpu.VMEM((nodes,) + small, jnp.float32),
            dma((chips,)), dma((chips,)), dma((chips,)), dma((chips,)),
            dma((parts,)), dma((parts,)), dma((nodes,)), dma((nodes,)),
        ],
        compiler_params=pltpu.CompilerParams(
            collective_id=1, has_side_effects=True, vmem_limit_bytes=40 << 20
        ),
        name="scatter_nodes",
    )(partial, norm, sums)


def on_device(feats, tiles, dst_block, src_block, tile_counts, norm, weight, bias, cotangent):
    rows, feat_local = feats.shape
    hid_local = cotangent.shape[1]
    nodes, parts = lax.axis_size("nodes"), lax.axis_size("feat")
    quarter = rows // parts
    norm_row = norm[None, :]
    counts, src, dst = tile_counts, src_block[0], dst_block[0]
    cot = lax.all_to_all(cotangent.T, "feat", 1, 0, tiled=True)
    bias_columns = jnp.broadcast_to(bias[:, None], (hid_local, 128))
    shards, full_weight, full_bias = gather_nodes(
        feats.T, norm_row, weight, bias_columns, nodes, parts
    )
    full_weight = full_weight.reshape(parts * feat_local, -1)
    full_bias = full_bias[:, :, 0].reshape(-1)
    aggregated = forward_tiles(counts, src, dst, tiles, shards, norm_row)
    agg = lax.all_to_all(aggregated, "feat", 1, 0, tiled=True)
    pre = (
        lax.dot_general(full_weight, agg, (((0,), (0,)), ((), ())), preferred_element_type=jnp.float32)
        + full_bias[:, None]
    )
    sigma = jax.nn.sigmoid(pre)
    hidden = (pre * sigma).astype(jnp.bfloat16)
    grad_pre = (cot.astype(jnp.float32) * (sigma * (1.0 + pre * (1.0 - sigma)))).astype(jnp.bfloat16)
    norm_part = lax.dynamic_slice_in_dim(norm_row, lax.axis_index("feat") * quarter, quarter, 1)
    back = (
        norm_part * lax.dot_general(full_weight, grad_pre, NN, preferred_element_type=jnp.float32)
    ).astype(jnp.bfloat16)
    back = lax.all_to_all(back, "feat", 0, 1, tiled=True)
    partial = backward_tiles(counts, src, dst, tiles, back)
    hidden = lax.all_to_all(hidden, "feat", 0, 1, tiled=True)
    scale = (rows * nodes) ** (-0.5)
    weight_part = lax.dot_general(agg, grad_pre, NT, preferred_element_type=jnp.float32)
    bias_part = jnp.sum(grad_pre, axis=1, dtype=jnp.float32)
    hid = weight.shape[1]
    sums = jnp.concatenate(
        [
            weight_part.reshape(parts, feat_local, hid),
            jnp.broadcast_to(bias_part[None, None, :], (parts, 8, hid)),
        ],
        axis=1,
    )
    grad_feats, sums = scatter_nodes(partial, norm_row, sums, parts, scale)
    grad_weight = sums[:feat_local]
    grad_bias = lax.dynamic_slice_in_dim(
        sums[feat_local], lax.axis_index("feat") * hid_local, hid_local, 0
    )
    return (hidden.T, grad_weight, grad_bias, grad_feats.T)


def solution(mesh):
    return jax.shard_map(
        on_device,
        mesh=mesh,
        in_specs=(
            P("nodes", "feat"),
            P("nodes", None, None, None, None),
            P("nodes", None, None),
            P("nodes", None, None),
            P("nodes", None),
            P("nodes"),
            P("feat", None),
            P("feat"),
            P("nodes", "feat"),
        ),
        out_specs=(P("nodes", "feat"), P("feat", None), P("feat"), P("nodes", "feat")),
        check_vma=False,
    )
```

```python
import functools

import jax
import jax.numpy as jnp
from jax import lax
from jax.experimental import pallas as pl
from jax.experimental.pallas import tpu as pltpu
from jax.sharding import PartitionSpec as P

GROUP = 4
NT = (((1,), (1,)), ((), ()))
NN = (((1,), (0,)), ((), ()))


def tile_products(n, tiles_ref, x_of, reads, writes, acc, dims):
    size = tiles_ref.shape[-1]
    slots = tiles_ref.shape[2]
    width = GROUP if slots % GROUP == 0 else 1

    def group(g, carry):
        products = []
        for k in range(width):
            slot = g * width + k
            x = x_of(pl.ds(pl.multiple_of(reads(slot) * size, size), size))
            x = jnp.where(slot < n, x, jnp.zeros_like(x))
            products.append(
                lax.dot_general(x, tiles_ref[0, 0, slot], dims, preferred_element_type=jnp.float32)
            )
        for k in range(width):
            place = writes(g * width + k)
            acc[place] = acc[place] + products[k]
        return carry

    lax.fori_loop(0, (n + width - 1) // width, group, 0)


def forward_kernel(counts, src, dst, tiles_ref, x_ref, norm_ref, out_ref, acc):
    peer = pl.program_id(0)
    size = tiles_ref.shape[-1]

    @pl.when(peer == 0)
    def _():
        acc[...] = jnp.zeros_like(acc)

    tile_products(
        counts[0, peer],
        tiles_ref,
        lambda cut: x_ref[0, :, cut],
        lambda slot: src[peer, slot],
        lambda slot: dst[peer, slot],
        acc,
        NT,
    )

    @pl.when(peer == pl.num_programs(0) - 1)
    def _():
        for b in range(acc.shape[0]):
            cut = slice(b * size, (b + 1) * size)
            out_ref[:, cut] = (norm_ref[:, cut] * acc[b]).astype(out_ref.dtype)


def backward_kernel(counts, src, dst, tiles_ref, x_ref, out_ref, acc):
    peer = pl.program_id(0)
    size = tiles_ref.shape[-1]
    acc[...] = jnp.zeros_like(acc)
    tile_products(
        counts[0, peer],
        tiles_ref,
        lambda cut: x_ref[:, cut],
        lambda slot: dst[peer, slot],
        lambda slot: src[peer, slot],
        acc,
        NN,
    )
    for b in range(acc.shape[0]):
        out_ref[0, :, b * size : (b + 1) * size] = acc[b].astype(out_ref.dtype)


def forward_tiles(counts, src, dst, tiles, x, norm):
    _, slabs, slots, size, _ = tiles.shape
    feat, rows = x.shape[1:]
    return pl.pallas_call(
        forward_kernel,
        grid_spec=pltpu.PrefetchScalarGridSpec(
            num_scalar_prefetch=3,
            grid=(slabs,),
            in_specs=[
                pl.BlockSpec((1, 1, slots, size, size), lambda p, *_: (0, p, 0, 0, 0)),
                pl.BlockSpec((1, feat, rows), lambda p, *_: (p, 0, 0)),
                pl.BlockSpec((1, rows), lambda p, *_: (0, 0)),
            ],
            out_specs=pl.BlockSpec((feat, rows), lambda p, *_: (0, 0)),
            scratch_shapes=[pltpu.VMEM((rows // size, feat, size), jnp.float32)],
        ),
        out_shape=jax.ShapeDtypeStruct((feat, rows), jnp.bfloat16),
        compiler_params=pltpu.CompilerParams(vmem_limit_bytes=60 << 20),
        name="forward_tiles",
    )(counts, src, dst, tiles, x, norm)


def backward_tiles(counts, src, dst, tiles, x):
    _, slabs, slots, size, _ = tiles.shape
    feat, rows = x.shape
    return pl.pallas_call(
        backward_kernel,
        grid_spec=pltpu.PrefetchScalarGridSpec(
            num_scalar_prefetch=3,
            grid=(slabs,),
            in_specs=[
                pl.BlockSpec((1, 1, slots, size, size), lambda p, *_: (0, p, 0, 0, 0)),
                pl.BlockSpec((feat, rows), lambda p, *_: (0, 0)),
            ],
            out_specs=pl.BlockSpec((1, feat, rows), lambda p, *_: (p, 0, 0)),
            scratch_shapes=[pltpu.VMEM((rows // size, feat, size), jnp.float32)],
        ),
        out_shape=jax.ShapeDtypeStruct((slabs, feat, rows), jnp.bfloat16),
        compiler_params=pltpu.CompilerParams(vmem_limit_bytes=60 << 20),
        name="backward_tiles",
    )(counts, src, dst, tiles, x)


def remote(src, dst, send, recv, target):
    return pltpu.make_async_remote_copy(
        src_ref=src,
        dst_ref=dst,
        send_sem=send,
        recv_sem=recv,
        device_id=target,
        device_id_type=pl.DeviceIdType.MESH,
    )


def greet(targets):
    barrier = pltpu.get_barrier_semaphore()
    for target in targets:
        pl.semaphore_signal(
            barrier, inc=1, device_id=target, device_id_type=pl.DeviceIdType.MESH
        )
    pl.semaphore_wait(barrier, len(targets))


def gather_kernel(
    nodes, parts, pieces,
    feats_ref, norm_ref, weight_ref, bias_ref, cot_ref,
    out_ref, weight_out, bias_out, cot_out,
    scaled, own_sem, send_sem, recv_sem, pass_send, pass_recv, small_send, small_recv,
):
    node, part = lax.axis_index("nodes"), lax.axis_index("feat")
    chips = nodes // 2
    chip, core = node // 2, node % 2
    sibling = {"nodes": chip * 2 + 1 - core}
    width = scaled.shape[1] // pieces
    cuts = [pl.ds(k * width, width) for k in range(pieces)]
    chip_at = lambda d: (chip + d) % chips
    node_at = lambda d: {"nodes": chip_at(d) * 2 + core}
    part_at = lambda d: {"feat": (part + d) % parts}
    greet([sibling] + [node_at(d) for d in range(1, chips)] + [part_at(d) for d in range(1, parts)])

    quarter = cot_ref.shape[1] // parts
    quarter_at = lambda d: pl.ds(pl.multiple_of((part + d) % parts * quarter, quarter), quarter)
    started = []
    own_cot = pltpu.make_async_copy(cot_ref.at[:, quarter_at(0)], cot_out.at[part], own_sem.at[pieces])
    own_cot.start()
    for d in range(1, parts):
        moves = (
            (weight_ref, weight_out),
            (bias_ref, bias_out),
            (cot_ref.at[:, quarter_at(d)], cot_out),
        )
        for k, (src, dst) in enumerate(moves):
            copy = remote(src, dst.at[part], small_send.at[d, k], small_recv.at[d, k], part_at(d))
            copy.start()
            started.append(copy)
    weight_out[part] = weight_ref[...]
    bias_out[part] = bias_ref[...]

    direct = {}
    own = []
    passed = []
    for k, cut in enumerate(cuts):
        scaled[:, cut] = (norm_ref[:, cut] * feats_ref[:, cut].astype(jnp.float32)).astype(scaled.dtype)
        place = out_ref.at[node, :, cut]
        for d in range(1, chips):
            copy = remote(scaled.at[:, cut], place, send_sem.at[d, k], recv_sem.at[d, k], node_at(d))
            copy.start()
            direct[d, k] = copy
        copy = remote(scaled.at[:, cut], place, pass_send.at[0, k], pass_recv.at[0, k], sibling)
        copy.start()
        passed.append(copy)
        copy = pltpu.make_async_copy(scaled.at[:, cut], place, own_sem.at[k])
        copy.start()
        own.append(copy)
    for k, cut in enumerate(cuts):
        for d in range(1, chips):
            direct[d, k].wait_recv()
            place = out_ref.at[chip_at(chips - d) * 2 + core, :, cut]
            copy = remote(place, place, pass_send.at[d, k], pass_recv.at[d, k], sibling)
            copy.start()
            passed.append(copy)
    for copy in own + [own_cot]:
        copy.wait()
    for copy in started + passed:
        copy.wait()
    for copy in direct.values():
        copy.wait_send()


def gather_nodes(feats, norm, weight, bias, cot, nodes, parts, pieces=4):
    feat, rows = feats.shape
    dma = pltpu.SemaphoreType.DMA
    chips = nodes // 2
    vmem = pl.BlockSpec(memory_space=pltpu.VMEM)
    return pl.pallas_call(
        functools.partial(gather_kernel, nodes, parts, pieces),
        out_shape=(
            jax.ShapeDtypeStruct((nodes, feat, rows), jnp.bfloat16),
            jax.ShapeDtypeStruct((parts,) + weight.shape, weight.dtype),
            jax.ShapeDtypeStruct((parts,) + bias.shape, bias.dtype),
            jax.ShapeDtypeStruct((parts, cot.shape[0], rows // parts), cot.dtype),
        ),
        in_specs=[vmem] * 4 + [pl.BlockSpec(memory_space=pl.ANY)],
        out_specs=(pl.BlockSpec(memory_space=pl.ANY), vmem, vmem, pl.BlockSpec(memory_space=pl.ANY)),
        scratch_shapes=[
            pltpu.VMEM((feat, rows), jnp.bfloat16),
            dma((pieces + 1,)),
            dma((chips, pieces)),
            dma((chips, pieces)),
            dma((chips, pieces)),
            dma((chips, pieces)),
            dma((parts, 3)),
            dma((parts, 3)),
        ],
        compiler_params=pltpu.CompilerParams(
            collective_id=0, has_side_effects=True, vmem_limit_bytes=60 << 20
        ),
        name="gather_nodes",
    )(feats, norm, weight, bias, cot)


def scatter_kernel(
    nodes, parts, scale,
    partial_ref, norm_ref, sums_ref, hidden_ref,
    out_ref, sums_out, hidden_out,
    sibling_buf, stage, arrived, small_part, small_stage, small_node,
    pass_send, pass_recv, send_sem, recv_sem, ps_send, ps_recv, ns_send, ns_recv,
    hid_send, hid_recv, own_sem,
):
    node, part = lax.axis_index("nodes"), lax.axis_index("feat")
    chips = nodes // 2
    chip, core = node // 2, node % 2
    rows = partial_ref.shape[2]
    step = min(rows, 1024)
    other = chip * 2 + 1 - core
    chip_at = lambda d: (chip + d) % chips
    node_at = lambda d: {"nodes": chip_at(d) * 2 + core}
    any_node = lambda d: {"nodes": (node + d) % nodes}
    part_at = lambda d: {"feat": (part + d) % parts}
    greet([any_node(d) for d in range(1, nodes)] + [part_at(d) for d in range(1, parts)])

    part_copies = []
    for d in range(1, parts):
        copy = remote(
            sums_ref.at[(part + d) % parts], small_part.at[d], ps_send.at[d], ps_recv.at[d], part_at(d)
        )
        copy.start()
        part_copies.append(copy)
    order = list(range(1, chips)) + [0]
    passes = {}
    for d in order:
        copy = remote(
            partial_ref.at[chip_at(d) * 2 + 1 - core],
            sibling_buf.at[d],
            pass_send.at[d],
            pass_recv.at[d],
            {"nodes": other},
        )
        copy.start()
        passes[d] = copy
    quarter = rows // parts
    mine_cut = pl.ds(pl.multiple_of(part * quarter, quarter), quarter)
    hidden_copies = []
    for d in range(1, parts):
        copy = remote(
            hidden_ref.at[(part + d) % parts],
            hidden_out.at[:, mine_cut],
            hid_send.at[d],
            hid_recv.at[d],
            part_at(d),
        )
        copy.start()
        hidden_copies.append(copy)
    own_hidden = pltpu.make_async_copy(hidden_ref.at[part], hidden_out.at[:, mine_cut], own_sem)
    own_hidden.start()

    for copy in part_copies:
        copy.wait_recv()
    small_stage[...] = sums_ref[part]
    for d in range(1, parts):
        small_stage[...] += small_part[d]
    node_copies = []
    for d in range(1, nodes):
        copy = remote(small_stage, small_node.at[node], ns_send.at[d], ns_recv.at[d], any_node(d))
        copy.start()
        node_copies.append(copy)

    directs = []
    for d in order:
        passes[d].wait_recv()
        mine = chip_at(d) * 2 + core

        @pl.loop(0, rows // step)
        def _(i):
            cut = pl.ds(pl.multiple_of(i * step, step), step)
            total = partial_ref[mine, :, cut].astype(jnp.float32) + sibling_buf[d, :, cut].astype(jnp.float32)
            if d == 0:
                out_ref[:, cut] = total
            else:
                stage[d, :, cut] = total.astype(stage.dtype)

        if d:
            copy = remote(stage.at[d], arrived.at[d], send_sem.at[d], recv_sem.at[d], node_at(d))
            copy.start()
            directs.append(copy)
    for copy in node_copies:
        copy.wait_recv()
    small_node[node] = small_stage[...]
    total = small_node[0]
    for d in range(1, nodes):
        total = total + small_node[d]
    sums_out[...] = total * scale
    for copy in directs:
        copy.wait_recv()

    @pl.loop(0, rows // step)
    def _(i):
        cut = pl.ds(pl.multiple_of(i * step, step), step)
        total = out_ref[:, cut]
        for d in range(1, chips):
            total = total + arrived[d, :, cut].astype(jnp.float32)
        out_ref[:, cut] = norm_ref[:, cut] * total

    own_hidden.wait()
    for copy in hidden_copies:
        copy.wait()
    for copy in part_copies + node_copies + list(passes.values()) + directs:
        copy.wait_send()


def scatter_nodes(partial, norm, sums, hidden, parts, scale):
    nodes, feat, rows = partial.shape
    dma = pltpu.SemaphoreType.DMA
    chips = nodes // 2
    vmem = pl.BlockSpec(memory_space=pltpu.VMEM)
    big = pltpu.VMEM((chips, feat, rows), jnp.bfloat16)
    small = sums.shape[1:]
    return pl.pallas_call(
        functools.partial(scatter_kernel, nodes, parts, scale),
        out_shape=(
            jax.ShapeDtypeStruct((feat, rows), jnp.float32),
            jax.ShapeDtypeStruct(small, jnp.float32),
            jax.ShapeDtypeStruct((hidden.shape[1], rows), hidden.dtype),
        ),
        in_specs=[vmem] * 4,
        out_specs=(vmem, vmem, vmem),
        scratch_shapes=[
            big, big, big,
            pltpu.VMEM((parts,) + small, jnp.float32),
            pltpu.VMEM(small, jnp.float32),
            pltpu.VMEM((nodes,) + small, jnp.float32),
            dma((chips,)), dma((chips,)), dma((chips,)), dma((chips,)),
            dma((parts,)), dma((parts,)), dma((nodes,)), dma((nodes,)),
            dma((parts,)), dma((parts,)), dma,
        ],
        compiler_params=pltpu.CompilerParams(
            collective_id=1, has_side_effects=True, vmem_limit_bytes=60 << 20
        ),
        name="scatter_nodes",
    )(partial, norm, sums, hidden)


def middle_kernel(
    parts, pieces,
    agg_ref, weight_ref, bias_ref, cot_ref, norm_ref,
    back_out, hidden_out, sums_out,
    agg, grad_pre, stage, in_send, in_recv, out_send, out_recv,
):
    part = lax.axis_index("feat")
    _, feat, quarter = agg.shape
    width = quarter // pieces
    hid_local = cot_ref.shape[1]
    hid = parts * hid_local
    part_at = lambda d: {"feat": (part + d) % parts}
    at = lambda d, k: pl.ds(
        pl.multiple_of((part + d) % parts * quarter + k * width, width), width
    )
    cuts = [pl.ds(k * width, width) for k in range(pieces)]
    greet([part_at(d) for d in range(1, parts)])

    arriving = {}
    for k, cut in enumerate(cuts):
        for d in range(1, parts):
            copy = remote(
                agg_ref.at[:, at(d, k)], agg.at[part, :, cut], in_send.at[d, k], in_recv.at[d, k], part_at(d)
            )
            copy.start()
            arriving[d, k] = copy
    for k, cut in enumerate(cuts):
        agg[part, :, cut] = agg_ref[:, at(0, k)]

    leaving = []
    for k, cut in enumerate(cuts):
        for d in range(1, parts):
            arriving[d, k].wait_recv()
        columns = agg[:, :, cut].reshape(parts * feat, width)
        pre = (
            lax.dot_general(
                weight_ref[...], columns, (((0,), (0,)), ((), ())), preferred_element_type=jnp.float32
            )
            + bias_ref[:, :1]
        )
        sigma = jax.nn.sigmoid(pre)
        hidden_out[:, :, cut] = (pre * sigma).astype(jnp.bfloat16).reshape(parts, hid_local, width)
        cot = cot_ref[:, :, cut].reshape(hid, width).astype(jnp.float32)
        grad = (cot * (sigma * (1.0 + pre * (1.0 - sigma)))).astype(jnp.bfloat16)
        grad_pre[:, cut] = grad
        back = norm_ref[:, at(0, k)] * lax.dot_general(
            weight_ref[...], grad, NN, preferred_element_type=jnp.float32
        )
        stage[:, :, cut] = back.astype(jnp.bfloat16).reshape(parts, feat, width)
        for d in range(1, parts):
            copy = remote(
                stage.at[(part + d) % parts, :, cut], back_out.at[:, at(0, k)],
                out_send.at[d, k], out_recv.at[d, k], part_at(d),
            )
            copy.start()
            leaving.append(copy)
        back_out[:, at(0, k)] = stage[part, :, cut]

    grads = grad_pre[...]
    sums_out[:, :feat] = lax.dot_general(
        agg[...].reshape(parts * feat, quarter), grads, NT, preferred_element_type=jnp.float32
    ).reshape(parts, feat, hid)
    bias_rows = lax.dot_general(
        jnp.ones((8, quarter), jnp.bfloat16), grads, NT, preferred_element_type=jnp.float32
    )
    for d in range(parts):
        sums_out[d, feat:] = bias_rows
    for copy in arriving.values():
        copy.wait_send()
    for copy in leaving:
        copy.wait()


def middle(aggregated, weight, bias, cot, norm, pieces=4):
    feat, rows = aggregated.shape
    parts, hid_local, quarter = cot.shape
    hid = parts * hid_local
    dma = pltpu.SemaphoreType.DMA((parts, pieces))
    vmem = pl.BlockSpec(memory_space=pltpu.VMEM)
    return pl.pallas_call(
        functools.partial(middle_kernel, parts, pieces),
        out_shape=(
            jax.ShapeDtypeStruct((feat, rows), jnp.bfloat16),
            jax.ShapeDtypeStruct(cot.shape, jnp.bfloat16),
            jax.ShapeDtypeStruct((parts, feat + 8, hid), jnp.float32),
        ),
        in_specs=[vmem] * 5,
        out_specs=(vmem, vmem, vmem),
        scratch_shapes=[
            pltpu.VMEM((parts, feat, quarter), jnp.bfloat16),
            pltpu.VMEM((hid, quarter), jnp.bfloat16),
            pltpu.VMEM((parts, feat, quarter), jnp.bfloat16),
            dma, dma, dma, dma,
        ],
        compiler_params=pltpu.CompilerParams(
            collective_id=2, has_side_effects=True, vmem_limit_bytes=60 << 20
        ),
        name="middle",
    )(aggregated, weight, bias, cot, norm)


def on_device(feats, tiles, dst_block, src_block, tile_counts, norm, weight, bias, cotangent):
    rows, feat_local = feats.shape
    hid_local = cotangent.shape[1]
    nodes, parts = lax.axis_size("nodes"), lax.axis_size("feat")
    norm_row = norm[None, :]
    counts, src, dst = tile_counts, src_block[0], dst_block[0]
    bias_columns = jnp.broadcast_to(bias[:, None], (hid_local, 128))
    shards, full_weight, full_bias, cot = gather_nodes(
        feats.T, norm_row, weight, bias_columns, cotangent.T, nodes, parts
    )
    full_weight = full_weight.reshape(parts * feat_local, -1)
    full_bias = full_bias.reshape(parts * hid_local, 128)
    aggregated = forward_tiles(counts, src, dst, tiles, shards, norm_row)
    back, hidden, sums = middle(aggregated, full_weight, full_bias, cot, norm_row)
    partial = backward_tiles(counts, src, dst, tiles, back)
    scale = (rows * nodes) ** (-0.5)
    grad_feats, sums, hidden = scatter_nodes(partial, norm_row, sums, hidden, parts, scale)
    grad_weight = sums[:feat_local]
    grad_bias = lax.dynamic_slice_in_dim(
        sums[feat_local], lax.axis_index("feat") * hid_local, hid_local, 0
    )
    return (hidden.T, grad_weight, grad_bias, grad_feats.T)


def solution(mesh):
    return jax.shard_map(
        on_device,
        mesh=mesh,
        in_specs=(
            P("nodes", "feat"),
            P("nodes", None, None, None, None),
            P("nodes", None, None),
            P("nodes", None, None),
            P("nodes", None),
            P("nodes"),
            P("feat", None),
            P("feat"),
            P("nodes", "feat"),
        ),
        out_specs=(P("nodes", "feat"), P("feat", None), P("feat"), P("nodes", "feat")),
        check_vma=False,
    )
```

```python
import functools

import jax
import jax.numpy as jnp
from jax import lax
from jax.experimental import pallas as pl
from jax.experimental.pallas import tpu as pltpu
from jax.sharding import PartitionSpec as P

GROUP = 8
NT = (((1,), (1,)), ((), ()))
NN = (((1,), (0,)), ((), ()))


def tile_copies(counts, slab, tiles_hbm, tiles_ref, sems, act):
    width = tiles_ref.shape[1] // sems.shape[1]
    for g in range(sems.shape[1]):

        @pl.when(g * width < counts[0, slab])
        def _():
            cut = pl.ds(g * width, width)
            act(
                pltpu.make_async_copy(
                    tiles_hbm.at[0, slab, cut], tiles_ref.at[slab, cut], sems.at[slab, g]
                )
            )


def tile_products(n, slab, tiles_ref, x_of, reads, writes, acc, dims):
    slots, size = tiles_ref.shape[1:3]
    width = GROUP if slots % GROUP == 0 else 1

    def group(g, carry):
        products = []
        for k in range(width):
            slot = g * width + k
            x = x_of(pl.ds(pl.multiple_of(reads(slot) * size, size), size))
            x = jnp.where(slot < n, x, jnp.zeros_like(x))
            products.append(
                lax.dot_general(x, tiles_ref[slab, slot], dims, preferred_element_type=jnp.float32)
            )
        for k in range(width):
            place = writes(g * width + k)
            acc[place] = acc[place] + products[k]
        return carry

    lax.fori_loop(0, (n + width - 1) // width, group, 0)


def forward_kernel(counts, src, dst, tiles_hbm, x_hbm, norm_ref, out_ref, tiles_ref, x_ref, acc, sems, x_sems):
    slabs = tiles_ref.shape[0]
    size = tiles_ref.shape[2]

    @pl.loop(0, slabs)
    def _(p):
        pltpu.make_async_copy(x_hbm.at[p], x_ref.at[p], x_sems.at[p]).start()
        tile_copies(counts, p, tiles_hbm, tiles_ref, sems, lambda copy: copy.start())

    acc[...] = jnp.zeros_like(acc)

    @pl.loop(0, slabs)
    def _(p):
        pltpu.make_async_copy(x_hbm.at[p], x_ref.at[p], x_sems.at[p]).wait()
        tile_copies(counts, p, tiles_hbm, tiles_ref, sems, lambda copy: copy.wait())
        tile_products(
            counts[0, p],
            p,
            tiles_ref,
            lambda cut: x_ref[p, :, cut],
            lambda slot: src[p, slot],
            lambda slot: dst[p, slot],
            acc,
            NT,
        )

    for b in range(acc.shape[0]):
        cut = slice(b * size, (b + 1) * size)
        out_ref[:, cut] = (norm_ref[:, cut] * acc[b]).astype(out_ref.dtype)


def backward_kernel(counts, src, dst, tiles_hbm, x_ref, out_hbm, tiles_ref, out_ref, acc, sems, out_sems):
    slabs = tiles_ref.shape[0]
    size = tiles_ref.shape[2]

    @pl.loop(0, slabs)
    def _(p):
        tile_copies(counts, p, tiles_hbm, tiles_ref, sems, lambda copy: copy.start())

    @pl.loop(0, slabs)
    def _(p):
        tile_copies(counts, p, tiles_hbm, tiles_ref, sems, lambda copy: copy.wait())
        acc[...] = jnp.zeros_like(acc)
        tile_products(
            counts[0, p],
            p,
            tiles_ref,
            lambda cut: x_ref[:, cut],
            lambda slot: dst[p, slot],
            lambda slot: src[p, slot],
            acc,
            NN,
        )
        for b in range(acc.shape[0]):
            out_ref[p, :, b * size : (b + 1) * size] = acc[b].astype(out_ref.dtype)
        pltpu.make_async_copy(out_ref.at[p], out_hbm.at[p], out_sems.at[p]).start()

    @pl.loop(0, slabs)
    def _(p):
        pltpu.make_async_copy(out_ref.at[p], out_hbm.at[p], out_sems.at[p]).wait()


def tile_call(kernel, name, counts, src, dst, tiles, rest, rest_specs, out_shape, out_spec, middle_shape, rows, feat):
    _, slabs, slots, size, _ = tiles.shape
    smem = pl.BlockSpec(memory_space=pltpu.SMEM)
    groups = slots // GROUP if slots % GROUP == 0 else 1
    return pl.pallas_call(
        kernel,
        out_shape=jax.ShapeDtypeStruct(out_shape, jnp.bfloat16),
        in_specs=[smem] * 3 + [pl.BlockSpec(memory_space=pl.ANY)] + rest_specs,
        out_specs=out_spec,
        scratch_shapes=[
            pltpu.VMEM((slabs, slots, size, size), jnp.bfloat16),
            pltpu.VMEM(middle_shape, jnp.bfloat16),
            pltpu.VMEM((rows // size, feat, size), jnp.float32),
            pltpu.SemaphoreType.DMA((slabs, groups)),
            pltpu.SemaphoreType.DMA((slabs,)),
        ],
        compiler_params=pltpu.CompilerParams(vmem_limit_bytes=60 << 20),
        name=name,
    )(counts, src, dst, tiles, *rest)


def forward_tiles(counts, src, dst, tiles, x, norm):
    _, feat, rows = x.shape
    vmem, hbm = pl.BlockSpec(memory_space=pltpu.VMEM), pl.BlockSpec(memory_space=pl.ANY)
    return tile_call(
        forward_kernel, "forward_tiles", counts, src, dst, tiles, (x, norm), [hbm, vmem],
        (feat, rows), vmem, x.shape, rows, feat,
    )


def backward_tiles(counts, src, dst, tiles, x):
    feat, rows = x.shape
    vmem, hbm = pl.BlockSpec(memory_space=pltpu.VMEM), pl.BlockSpec(memory_space=pl.ANY)
    shape = (tiles.shape[1], feat, rows)
    return tile_call(
        backward_kernel, "backward_tiles", counts, src, dst, tiles, (x,), [vmem],
        shape, hbm, shape, rows, feat,
    )


def remote(src, dst, send, recv, target):
    return pltpu.make_async_remote_copy(
        src_ref=src,
        dst_ref=dst,
        send_sem=send,
        recv_sem=recv,
        device_id=target,
        device_id_type=pl.DeviceIdType.MESH,
    )


def greet(targets):
    barrier = pltpu.get_barrier_semaphore()
    for target in targets:
        pl.semaphore_signal(
            barrier, inc=1, device_id=target, device_id_type=pl.DeviceIdType.MESH
        )
    pl.semaphore_wait(barrier, len(targets))


def gather_kernel(
    nodes, parts, pieces,
    feats_ref, norm_ref, weight_ref, bias_ref, cot_ref,
    out_ref, weight_out, bias_out, cot_out,
    scaled, own_sem, send_sem, recv_sem, pass_send, pass_recv, small_send, small_recv,
):
    node, part = lax.axis_index("nodes"), lax.axis_index("feat")
    chips = nodes // 2
    chip, core = node // 2, node % 2
    sibling = {"nodes": chip * 2 + 1 - core}
    width = scaled.shape[1] // pieces
    cuts = [pl.ds(k * width, width) for k in range(pieces)]
    chip_at = lambda d: (chip + d) % chips
    node_at = lambda d: {"nodes": chip_at(d) * 2 + core}
    part_at = lambda d: {"feat": (part + d) % parts}
    square = chips == 4
    over_x = chip + 1 - 2 * (chip % 2)
    over_y = (chip + 2) % 4
    across = over_y + 1 - 2 * (chip % 2)
    node_of = lambda q: {"nodes": q * 2 + core}
    peers = [node_of(over_x), node_of(over_y)] if square else [node_at(d) for d in range(1, chips)]
    greet([sibling] + peers + [part_at(d) for d in range(1, parts)])

    quarter = cot_ref.shape[1] // parts
    quarter_at = lambda d: pl.ds(pl.multiple_of((part + d) % parts * quarter, quarter), quarter)
    started = []
    own_cot = pltpu.make_async_copy(cot_ref.at[:, quarter_at(0)], cot_out.at[part], own_sem.at[pieces])
    own_cot.start()
    for d in range(1, parts):
        moves = (
            (weight_ref, weight_out),
            (bias_ref, bias_out),
            (cot_ref.at[:, quarter_at(d)], cot_out),
        )
        for k, (src, dst) in enumerate(moves):
            copy = remote(src, dst.at[part], small_send.at[d, k], small_recv.at[d, k], part_at(d))
            copy.start()
            started.append(copy)
    weight_out[part] = weight_ref[...]
    bias_out[part] = bias_ref[...]

    direct = {}
    own = []
    passed = []
    half = pieces // 2
    order_y = list(range(pieces))
    order_x = order_y[half:] + order_y[:half]

    def send(d, k, src, place, target):
        copy = remote(src, place, send_sem.at[d, k], recv_sem.at[d, k], target)
        copy.start()
        direct[d, k] = copy

    def hand_on(d, k, src, place):
        copy = remote(src, place, pass_send.at[d, k], pass_recv.at[d, k], sibling)
        copy.start()
        passed.append(copy)

    scaled[...] = (norm_ref[...] * feats_ref[...].astype(jnp.float32)).astype(scaled.dtype)
    for i in range(pieces):
        if square:
            for d, k, target in ((1, order_x[i], over_x), (2, order_y[i], over_y)):
                cut = cuts[k]
                send(d, k, scaled.at[:, cut], out_ref.at[node, :, cut], node_of(target))
        else:
            cut = cuts[i]
            for d in range(1, chips):
                send(d, i, scaled.at[:, cut], out_ref.at[node, :, cut], node_at(d))
    for k, cut in enumerate(cuts):
        place = out_ref.at[node, :, cut]
        hand_on(0, k, scaled.at[:, cut], place)
        copy = pltpu.make_async_copy(scaled.at[:, cut], place, own_sem.at[k])
        copy.start()
        own.append(copy)
    if square:
        for i in range(pieces):
            for d, k, source, other in (
                (1, order_x[i], over_x, over_y),
                (2, order_y[i], over_y, over_x),
            ):
                direct[d, k].wait_recv()
                place = out_ref.at[source * 2 + core, :, cuts[k]]
                if (k >= half) == (d == 1):
                    send(3, k, place, place, node_of(other))
                hand_on(d, k, place, place)
        for i in range(half):
            for k in (half + i, i):
                direct[3, k].wait_recv()
                place = out_ref.at[across * 2 + core, :, cuts[k]]
                hand_on(3, k, place, place)
    else:
        for k, cut in enumerate(cuts):
            for d in range(1, chips):
                direct[d, k].wait_recv()
                place = out_ref.at[chip_at(chips - d) * 2 + core, :, cut]
                hand_on(d, k, place, place)
    for copy in own + [own_cot]:
        copy.wait()
    for copy in started + passed:
        copy.wait()
    for copy in direct.values():
        copy.wait_send()


def gather_nodes(feats, norm, weight, bias, cot, nodes, parts, pieces=4):
    feat, rows = feats.shape
    dma = pltpu.SemaphoreType.DMA
    chips = nodes // 2
    vmem = pl.BlockSpec(memory_space=pltpu.VMEM)
    return pl.pallas_call(
        functools.partial(gather_kernel, nodes, parts, pieces),
        out_shape=(
            jax.ShapeDtypeStruct((nodes, feat, rows), jnp.bfloat16),
            jax.ShapeDtypeStruct((parts,) + weight.shape, weight.dtype),
            jax.ShapeDtypeStruct((parts,) + bias.shape, bias.dtype),
            jax.ShapeDtypeStruct((parts, cot.shape[0], rows // parts), cot.dtype),
        ),
        in_specs=[vmem] * 4 + [pl.BlockSpec(memory_space=pl.ANY)],
        out_specs=(pl.BlockSpec(memory_space=pl.ANY), vmem, vmem, pl.BlockSpec(memory_space=pl.ANY)),
        scratch_shapes=[
            pltpu.VMEM((feat, rows), jnp.bfloat16),
            dma((pieces + 1,)),
            dma((chips, pieces)),
            dma((chips, pieces)),
            dma((chips, pieces)),
            dma((chips, pieces)),
            dma((parts, 3)),
            dma((parts, 3)),
        ],
        compiler_params=pltpu.CompilerParams(
            collective_id=0, has_side_effects=True, vmem_limit_bytes=60 << 20
        ),
        name="gather_nodes",
    )(feats, norm, weight, bias, cot)


def scatter_kernel(
    nodes, parts, scale,
    partial_ref, norm_ref, sums_ref, hidden_ref,
    out_ref, sums_out, hidden_out,
    own_buf, sibling_buf, stage, arrived, small_part, small_stage, small_node,
    pass_send, pass_recv, send_sem, recv_sem, ps_send, ps_recv, ns_send, ns_recv,
    hid_send, hid_recv, own_sem,
):
    node, part = lax.axis_index("nodes"), lax.axis_index("feat")
    chips = nodes // 2
    chip, core = node // 2, node % 2
    rows = partial_ref.shape[2]
    other = chip * 2 + 1 - core
    chip_at = lambda d: (chip + d) % chips
    node_at = lambda d: {"nodes": chip_at(d) * 2 + core}
    square = chips == 4
    over_x = chip + 1 - 2 * (chip % 2)
    over_y = (chip + 2) % 4
    across = over_y + 1 - 2 * (chip % 2)
    node_of = lambda q: {"nodes": q * 2 + core}
    chip_of = (lambda d: (chip, over_x, over_y, across)[d]) if square else chip_at
    any_node = lambda d: {"nodes": (node + d) % nodes}
    part_at = lambda d: {"feat": (part + d) % parts}
    greet([any_node(d) for d in range(1, nodes)] + [part_at(d) for d in range(1, parts)])

    part_copies = []
    for d in range(1, parts):
        copy = remote(
            sums_ref.at[(part + d) % parts], small_part.at[d], ps_send.at[d], ps_recv.at[d], part_at(d)
        )
        copy.start()
        part_copies.append(copy)
    order = list(range(chips - 1, -1, -1))
    loads = {}
    passes = {}
    for d in order:
        copy = remote(
            partial_ref.at[chip_of(d) * 2 + 1 - core],
            sibling_buf.at[d],
            pass_send.at[d],
            pass_recv.at[d],
            {"nodes": other},
        )
        copy.start()
        passes[d] = copy
        load = pltpu.make_async_copy(
            partial_ref.at[chip_of(d) * 2 + core], own_buf.at[d], own_sem.at[d]
        )
        load.start()
        loads[d] = load
    quarter = rows // parts
    mine_cut = pl.ds(pl.multiple_of(part * quarter, quarter), quarter)
    hidden_copies = []
    for d in range(1, parts):
        copy = remote(
            hidden_ref.at[(part + d) % parts],
            hidden_out.at[:, mine_cut],
            hid_send.at[d],
            hid_recv.at[d],
            part_at(d),
        )
        copy.start()
        hidden_copies.append(copy)
    own_hidden = pltpu.make_async_copy(hidden_ref.at[part], hidden_out.at[:, mine_cut], own_sem.at[chips])
    own_hidden.start()

    directs = []

    def send(i, src, place, target):
        copy = remote(src, place, send_sem.at[i], recv_sem.at[i], node_of(target))
        copy.start()
        directs.append(copy)
        return copy

    def each(start, length, body):
        size = min(length, 1024)

        @pl.loop(0, length // size)
        def _(i):
            body(pl.ds(pl.multiple_of(start + i * size, size), size))

    half = rows // 2
    low, high = pl.ds(0, half), pl.ds(half, half)
    first = {}
    for d in order:
        loads[d].wait()
        passes[d].wait_recv()

        def join(cut, d=d):
            total = own_buf[d, :, cut].astype(jnp.float32) + sibling_buf[d, :, cut].astype(jnp.float32)
            if d == 0:
                out_ref[:, cut] = total
            else:
                stage[d, :, cut] = total.astype(stage.dtype)

        each(0, rows, join)
        if square:
            if d == 3:
                first["low"] = send(0, stage.at[3, :, low], arrived.at[1, :, low], over_y)
                first["high"] = send(1, stage.at[3, :, high], arrived.at[2, :, high], over_x)
            elif d == 2:
                send(2, stage.at[2, :, low], arrived.at[0, :, low], over_y)
            elif d == 1:
                send(3, stage.at[1, :, high], arrived.at[0, :, high], over_x)
        elif d:
            send(d, stage.at[d], arrived.at[d], chip_at(d))

    for copy in part_copies:
        copy.wait_recv()
    small_stage[...] = sums_ref[part]
    for d in range(1, parts):
        small_stage[...] += small_part[d]
    node_copies = []
    for d in range(1, nodes):
        copy = remote(small_stage, small_node.at[node], ns_send.at[d], ns_recv.at[d], any_node(d))
        copy.start()
        node_copies.append(copy)

    held = list(directs)
    if square:

        def add_stage(d):
            def body(cut):
                total = stage[d, :, cut].astype(jnp.float32) + arrived[d, :, cut].astype(jnp.float32)
                stage[d, :, cut] = total.astype(stage.dtype)

            return body

        first["low"].wait_recv()
        each(0, half, add_stage(1))
        send(4, stage.at[1, :, low], arrived.at[3, :, low], over_x)
        first["high"].wait_recv()
        each(half, half, add_stage(2))
        send(5, stage.at[2, :, high], arrived.at[3, :, high], over_y)
        held = directs[2:]
    for copy in node_copies:
        copy.wait_recv()
    small_node[node] = small_stage[...]
    total = small_node[0]
    for d in range(1, nodes):
        total = total + small_node[d]
    sums_out[...] = total * scale
    for copy in held:
        copy.wait_recv()

    def finish(cut):
        total = out_ref[:, cut]
        for d in (0, 3) if square else range(1, chips):
            total = total + arrived[d, :, cut].astype(jnp.float32)
        out_ref[:, cut] = norm_ref[:, cut] * total

    each(0, rows, finish)
    own_hidden.wait()
    for copy in hidden_copies:
        copy.wait()
    for copy in part_copies + node_copies + list(passes.values()) + directs:
        copy.wait_send()


def scatter_nodes(partial, norm, sums, hidden, parts, scale):
    nodes, feat, rows = partial.shape
    dma = pltpu.SemaphoreType.DMA
    chips = nodes // 2
    vmem = pl.BlockSpec(memory_space=pltpu.VMEM)
    big = pltpu.VMEM((chips, feat, rows), jnp.bfloat16)
    small = sums.shape[1:]
    return pl.pallas_call(
        functools.partial(scatter_kernel, nodes, parts, scale),
        out_shape=(
            jax.ShapeDtypeStruct((feat, rows), jnp.float32),
            jax.ShapeDtypeStruct(small, jnp.float32),
            jax.ShapeDtypeStruct((hidden.shape[1], rows), hidden.dtype),
        ),
        in_specs=[pl.BlockSpec(memory_space=pl.ANY)] + [vmem] * 3,
        out_specs=(vmem, vmem, vmem),
        scratch_shapes=[
            big, big, big, big,
            pltpu.VMEM((parts,) + small, jnp.float32),
            pltpu.VMEM(small, jnp.float32),
            pltpu.VMEM((nodes,) + small, jnp.float32),
            dma((chips,)), dma((chips,)), dma((max(chips, 6),)), dma((max(chips, 6),)),
            dma((parts,)), dma((parts,)), dma((nodes,)), dma((nodes,)),
            dma((parts,)), dma((parts,)), dma((chips + 1,)),
        ],
        compiler_params=pltpu.CompilerParams(
            collective_id=1, has_side_effects=True, vmem_limit_bytes=60 << 20
        ),
        name="scatter_nodes",
    )(partial, norm, sums, hidden)


def middle_kernel(
    parts, pieces,
    agg_ref, weight_ref, bias_ref, cot_ref, norm_ref,
    back_out, hidden_out, sums_out,
    agg, grad_pre, stage, in_send, in_recv, out_send, out_recv,
):
    part = lax.axis_index("feat")
    _, feat, quarter = agg.shape
    width = quarter // pieces
    hid_local = cot_ref.shape[1]
    hid = parts * hid_local
    part_at = lambda d: {"feat": (part + d) % parts}
    at = lambda d, k: pl.ds(
        pl.multiple_of((part + d) % parts * quarter + k * width, width), width
    )
    cuts = [pl.ds(k * width, width) for k in range(pieces)]
    greet([part_at(d) for d in range(1, parts)])

    arriving = {}
    for k, cut in enumerate(cuts):
        for d in range(1, parts):
            copy = remote(
                agg_ref.at[:, at(d, k)], agg.at[part, :, cut], in_send.at[d, k], in_recv.at[d, k], part_at(d)
            )
            copy.start()
            arriving[d, k] = copy
    for k, cut in enumerate(cuts):
        agg[part, :, cut] = agg_ref[:, at(0, k)]

    leaving = []
    for k, cut in enumerate(cuts):
        for d in range(1, parts):
            arriving[d, k].wait_recv()
        columns = agg[:, :, cut].reshape(parts * feat, width)
        pre = (
            lax.dot_general(
                weight_ref[...], columns, (((0,), (0,)), ((), ())), preferred_element_type=jnp.float32
            )
            + bias_ref[:, :1]
        )
        sigma = jax.nn.sigmoid(pre)
        hidden_out[:, :, cut] = (pre * sigma).astype(jnp.bfloat16).reshape(parts, hid_local, width)
        cot = cot_ref[:, :, cut].reshape(hid, width).astype(jnp.float32)
        grad = (cot * (sigma * (1.0 + pre * (1.0 - sigma)))).astype(jnp.bfloat16)
        grad_pre[:, cut] = grad
        back = norm_ref[:, at(0, k)] * lax.dot_general(
            weight_ref[...], grad, NN, preferred_element_type=jnp.float32
        )
        stage[:, :, cut] = back.astype(jnp.bfloat16).reshape(parts, feat, width)
        for d in range(1, parts):
            copy = remote(
                stage.at[(part + d) % parts, :, cut], back_out.at[:, at(0, k)],
                out_send.at[d, k], out_recv.at[d, k], part_at(d),
            )
            copy.start()
            leaving.append(copy)
        back_out[:, at(0, k)] = stage[part, :, cut]

    grads = grad_pre[...]
    sums_out[:, :feat] = lax.dot_general(
        agg[...].reshape(parts * feat, quarter), grads, NT, preferred_element_type=jnp.float32
    ).reshape(parts, feat, hid)
    bias_rows = lax.dot_general(
        jnp.ones((8, quarter), jnp.bfloat16), grads, NT, preferred_element_type=jnp.float32
    )
    for d in range(parts):
        sums_out[d, feat:] = bias_rows
    for copy in arriving.values():
        copy.wait_send()
    for copy in leaving:
        copy.wait()


def middle(aggregated, weight, bias, cot, norm, pieces=4):
    feat, rows = aggregated.shape
    parts, hid_local, quarter = cot.shape
    hid = parts * hid_local
    dma = pltpu.SemaphoreType.DMA((parts, pieces))
    vmem = pl.BlockSpec(memory_space=pltpu.VMEM)
    return pl.pallas_call(
        functools.partial(middle_kernel, parts, pieces),
        out_shape=(
            jax.ShapeDtypeStruct((feat, rows), jnp.bfloat16),
            jax.ShapeDtypeStruct(cot.shape, jnp.bfloat16),
            jax.ShapeDtypeStruct((parts, feat + 8, hid), jnp.float32),
        ),
        in_specs=[vmem] * 5,
        out_specs=(vmem, vmem, vmem),
        scratch_shapes=[
            pltpu.VMEM((parts, feat, quarter), jnp.bfloat16),
            pltpu.VMEM((hid, quarter), jnp.bfloat16),
            pltpu.VMEM((parts, feat, quarter), jnp.bfloat16),
            dma, dma, dma, dma,
        ],
        compiler_params=pltpu.CompilerParams(
            collective_id=2, has_side_effects=True, vmem_limit_bytes=60 << 20
        ),
        name="middle",
    )(aggregated, weight, bias, cot, norm)


def on_device(feats, tiles, dst_block, src_block, tile_counts, norm, weight, bias, cotangent):
    rows, feat_local = feats.shape
    hid_local = cotangent.shape[1]
    nodes, parts = lax.axis_size("nodes"), lax.axis_size("feat")
    norm_row = norm[None, :]
    counts, src, dst = tile_counts, src_block[0], dst_block[0]
    bias_columns = jnp.broadcast_to(bias[:, None], (hid_local, 128))
    shards, full_weight, full_bias, cot = gather_nodes(
        feats.T, norm_row, weight, bias_columns, cotangent.T, nodes, parts
    )
    full_weight = full_weight.reshape(parts * feat_local, -1)
    full_bias = full_bias.reshape(parts * hid_local, 128)
    aggregated = forward_tiles(counts, src, dst, tiles, shards, norm_row)
    back, hidden, sums = middle(aggregated, full_weight, full_bias, cot, norm_row)
    partial = backward_tiles(counts, src, dst, tiles, back)
    scale = (rows * nodes) ** (-0.5)
    grad_feats, sums, hidden = scatter_nodes(partial, norm_row, sums, hidden, parts, scale)
    grad_weight = sums[:feat_local]
    grad_bias = lax.dynamic_slice_in_dim(
        sums[feat_local], lax.axis_index("feat") * hid_local, hid_local, 0
    )
    return (hidden.T, grad_weight, grad_bias, grad_feats.T)


def solution(mesh):
    return jax.shard_map(
        on_device,
        mesh=mesh,
        in_specs=(
            P("nodes", "feat"),
            P("nodes", None, None, None, None),
            P("nodes", None, None),
            P("nodes", None, None),
            P("nodes", None),
            P("nodes"),
            P("feat", None),
            P("feat"),
            P("nodes", "feat"),
        ),
        out_specs=(P("nodes", "feat"), P("feat", None), P("feat"), P("nodes", "feat")),
        check_vma=False,
    )
```

```python
import functools

import jax
import jax.numpy as jnp
from jax import lax
from jax.experimental import pallas as pl
from jax.experimental.pallas import tpu as pltpu
from jax.sharding import PartitionSpec as P

GROUP = 8
NT = (((1,), (1,)), ((), ()))
NN = (((1,), (0,)), ((), ()))


def tile_copies(counts, slab, tiles_hbm, tiles_ref, sems, act):
    width = tiles_ref.shape[1] // sems.shape[1]
    for g in range(sems.shape[1]):

        @pl.when(g * width < counts[0, slab])
        def _():
            cut = pl.ds(g * width, width)
            act(
                pltpu.make_async_copy(
                    tiles_hbm.at[0, slab, cut], tiles_ref.at[slab, cut], sems.at[slab, g]
                )
            )


def tile_products(n, slab, tiles_ref, x_of, reads, writes, acc, dims):
    slots, size = tiles_ref.shape[1:3]
    width = GROUP if slots % GROUP == 0 else 1

    def group(g, carry):
        products = []
        for k in range(width):
            slot = g * width + k
            x = x_of(pl.ds(pl.multiple_of(reads(slot) * size, size), size))
            x = jnp.where(slot < n, x, jnp.zeros_like(x))
            products.append(
                lax.dot_general(x, tiles_ref[slab, slot], dims, preferred_element_type=jnp.float32)
            )
        for k in range(width):
            place = writes(g * width + k)
            acc[place] = acc[place] + products[k]
        return carry

    lax.fori_loop(0, (n + width - 1) // width, group, 0)


def forward_kernel(counts, src, dst, tiles_hbm, x_hbm, norm_ref, out_ref, tiles_ref, x_ref, acc, sems, x_sems):
    slabs = tiles_ref.shape[0]
    size = tiles_ref.shape[2]

    @pl.loop(0, slabs)
    def _(p):
        pltpu.make_async_copy(x_hbm.at[p], x_ref.at[p], x_sems.at[p]).start()
        tile_copies(counts, p, tiles_hbm, tiles_ref, sems, lambda copy: copy.start())

    acc[...] = jnp.zeros_like(acc)

    @pl.loop(0, slabs)
    def _(p):
        pltpu.make_async_copy(x_hbm.at[p], x_ref.at[p], x_sems.at[p]).wait()
        tile_copies(counts, p, tiles_hbm, tiles_ref, sems, lambda copy: copy.wait())
        tile_products(
            counts[0, p],
            p,
            tiles_ref,
            lambda cut: x_ref[p, :, cut],
            lambda slot: src[p, slot],
            lambda slot: dst[p, slot],
            acc,
            NT,
        )

    for b in range(acc.shape[0]):
        cut = slice(b * size, (b + 1) * size)
        out_ref[:, cut] = (norm_ref[:, cut] * acc[b]).astype(out_ref.dtype)


def backward_kernel(counts, src, dst, tiles_hbm, x_ref, out_hbm, tiles_ref, out_ref, acc, sems, out_sems):
    slabs = tiles_ref.shape[0]
    size = tiles_ref.shape[2]

    @pl.loop(0, slabs)
    def _(p):
        tile_copies(counts, p, tiles_hbm, tiles_ref, sems, lambda copy: copy.start())

    @pl.loop(0, slabs)
    def _(p):
        tile_copies(counts, p, tiles_hbm, tiles_ref, sems, lambda copy: copy.wait())
        acc[...] = jnp.zeros_like(acc)
        tile_products(
            counts[0, p],
            p,
            tiles_ref,
            lambda cut: x_ref[:, cut],
            lambda slot: dst[p, slot],
            lambda slot: src[p, slot],
            acc,
            NN,
        )
        for b in range(acc.shape[0]):
            out_ref[p, :, b * size : (b + 1) * size] = acc[b].astype(out_ref.dtype)
        pltpu.make_async_copy(out_ref.at[p], out_hbm.at[p], out_sems.at[p]).start()

    @pl.loop(0, slabs)
    def _(p):
        pltpu.make_async_copy(out_ref.at[p], out_hbm.at[p], out_sems.at[p]).wait()


def tile_call(kernel, name, counts, src, dst, tiles, rest, rest_specs, out_shape, out_spec, middle_shape, rows, feat):
    _, slabs, slots, size, _ = tiles.shape
    smem = pl.BlockSpec(memory_space=pltpu.SMEM)
    groups = slots // GROUP if slots % GROUP == 0 else 1
    return pl.pallas_call(
        kernel,
        out_shape=jax.ShapeDtypeStruct(out_shape, jnp.bfloat16),
        in_specs=[smem] * 3 + [pl.BlockSpec(memory_space=pl.ANY)] + rest_specs,
        out_specs=out_spec,
        scratch_shapes=[
            pltpu.VMEM((slabs, slots, size, size), jnp.bfloat16),
            pltpu.VMEM(middle_shape, jnp.bfloat16),
            pltpu.VMEM((rows // size, feat, size), jnp.float32),
            pltpu.SemaphoreType.DMA((slabs, groups)),
            pltpu.SemaphoreType.DMA((slabs,)),
        ],
        compiler_params=pltpu.CompilerParams(vmem_limit_bytes=60 << 20),
        name=name,
    )(counts, src, dst, tiles, *rest)


def forward_tiles(counts, src, dst, tiles, x, norm):
    _, feat, rows = x.shape
    vmem, hbm = pl.BlockSpec(memory_space=pltpu.VMEM), pl.BlockSpec(memory_space=pl.ANY)
    return tile_call(
        forward_kernel, "forward_tiles", counts, src, dst, tiles, (x, norm), [hbm, vmem],
        (feat, rows), vmem, x.shape, rows, feat,
    )


def backward_tiles(counts, src, dst, tiles, x):
    feat, rows = x.shape
    vmem, hbm = pl.BlockSpec(memory_space=pltpu.VMEM), pl.BlockSpec(memory_space=pl.ANY)
    shape = (tiles.shape[1], feat, rows)
    return tile_call(
        backward_kernel, "backward_tiles", counts, src, dst, tiles, (x,), [vmem],
        shape, hbm, shape, rows, feat,
    )


def remote(src, dst, send, recv, target):
    return pltpu.make_async_remote_copy(
        src_ref=src,
        dst_ref=dst,
        send_sem=send,
        recv_sem=recv,
        device_id=target,
        device_id_type=pl.DeviceIdType.MESH,
    )


def greet(targets):
    barrier = pltpu.get_barrier_semaphore()
    for target in targets:
        pl.semaphore_signal(
            barrier, inc=1, device_id=target, device_id_type=pl.DeviceIdType.MESH
        )
    pl.semaphore_wait(barrier, len(targets))


def gather_kernel(
    nodes, parts, pieces,
    feats_ref, norm_ref, weight_ref, bias_ref, cot_ref,
    out_ref, weight_out, bias_out, cot_out,
    scaled, own_sem, send_sem, recv_sem, pass_send, pass_recv, small_send, small_recv,
):
    node, part = lax.axis_index("nodes"), lax.axis_index("feat")
    chips = nodes // 2
    chip, core = node // 2, node % 2
    sibling = {"nodes": chip * 2 + 1 - core}
    width = scaled.shape[1] // pieces
    cuts = [pl.ds(k * width, width) for k in range(pieces)]
    chip_at = lambda d: (chip + d) % chips
    node_at = lambda d: {"nodes": chip_at(d) * 2 + core}
    part_at = lambda d: {"feat": (part + d) % parts}
    square = chips == 4
    over_x = chip + 1 - 2 * (chip % 2)
    over_y = (chip + 2) % 4
    across = over_y + 1 - 2 * (chip % 2)
    node_of = lambda q: {"nodes": q * 2 + core}
    peers = [node_of(over_x), node_of(over_y)] if square else [node_at(d) for d in range(1, chips)]
    greet([sibling] + peers + [part_at(d) for d in range(1, parts)])

    quarter = cot_ref.shape[1] // parts
    quarter_at = lambda d: pl.ds(pl.multiple_of((part + d) % parts * quarter, quarter), quarter)
    started = []
    own_cot = pltpu.make_async_copy(cot_ref.at[:, quarter_at(0)], cot_out.at[part], own_sem.at[pieces])
    own_cot.start()
    for d in range(1, parts):
        moves = (
            (weight_ref, weight_out),
            (bias_ref, bias_out),
            (cot_ref.at[:, quarter_at(d)], cot_out),
        )
        for k, (src, dst) in enumerate(moves):
            copy = remote(src, dst.at[part], small_send.at[d, k], small_recv.at[d, k], part_at(d))
            copy.start()
            started.append(copy)
    weight_out[part] = weight_ref[...]
    bias_out[part] = bias_ref[...]

    direct = {}
    own = []
    passed = []
    half = pieces // 2
    order_y = list(range(pieces))
    order_x = order_y[half:] + order_y[:half]

    def send(d, k, src, place, target):
        copy = remote(src, place, send_sem.at[d, k], recv_sem.at[d, k], target)
        copy.start()
        direct[d, k] = copy

    def hand_on(d, k, src, place):
        copy = remote(src, place, pass_send.at[d, k], pass_recv.at[d, k], sibling)
        copy.start()
        passed.append(copy)

    scaled[...] = (norm_ref[...] * feats_ref[...].astype(jnp.float32)).astype(scaled.dtype)
    for i in range(pieces):
        if square:
            for d, k, target in ((1, order_x[i], over_x), (2, order_y[i], over_y)):
                cut = cuts[k]
                send(d, k, scaled.at[:, cut], out_ref.at[node, :, cut], node_of(target))
        else:
            cut = cuts[i]
            for d in range(1, chips):
                send(d, i, scaled.at[:, cut], out_ref.at[node, :, cut], node_at(d))
    for k, cut in enumerate(cuts):
        place = out_ref.at[node, :, cut]
        hand_on(0, k, scaled.at[:, cut], place)
        copy = pltpu.make_async_copy(scaled.at[:, cut], place, own_sem.at[k])
        copy.start()
        own.append(copy)
    if square:
        for i in range(pieces):
            for d, k, source, other in (
                (1, order_x[i], over_x, over_y),
                (2, order_y[i], over_y, over_x),
            ):
                direct[d, k].wait_recv()
                place = out_ref.at[source * 2 + core, :, cuts[k]]
                if (k >= half) == (d == 1):
                    send(3, k, place, place, node_of(other))
                hand_on(d, k, place, place)
        for i in range(half):
            for k in (half + i, i):
                direct[3, k].wait_recv()
                place = out_ref.at[across * 2 + core, :, cuts[k]]
                hand_on(3, k, place, place)
    else:
        for k, cut in enumerate(cuts):
            for d in range(1, chips):
                direct[d, k].wait_recv()
                place = out_ref.at[chip_at(chips - d) * 2 + core, :, cut]
                hand_on(d, k, place, place)
    for copy in own + [own_cot]:
        copy.wait()
    for copy in started + passed:
        copy.wait()
    for copy in direct.values():
        copy.wait_send()


def gather_nodes(feats, norm, weight, bias, cot, nodes, parts, pieces=8):
    feat, rows = feats.shape
    dma = pltpu.SemaphoreType.DMA
    chips = nodes // 2
    vmem = pl.BlockSpec(memory_space=pltpu.VMEM)
    return pl.pallas_call(
        functools.partial(gather_kernel, nodes, parts, pieces),
        out_shape=(
            jax.ShapeDtypeStruct((nodes, feat, rows), jnp.bfloat16),
            jax.ShapeDtypeStruct((parts,) + weight.shape, weight.dtype),
            jax.ShapeDtypeStruct((parts,) + bias.shape, bias.dtype),
            jax.ShapeDtypeStruct((parts, cot.shape[0], rows // parts), cot.dtype),
        ),
        in_specs=[vmem] * 4 + [pl.BlockSpec(memory_space=pl.ANY)],
        out_specs=(pl.BlockSpec(memory_space=pl.ANY), vmem, vmem, pl.BlockSpec(memory_space=pl.ANY)),
        scratch_shapes=[
            pltpu.VMEM((feat, rows), jnp.bfloat16),
            dma((pieces + 1,)),
            dma((chips, pieces)),
            dma((chips, pieces)),
            dma((chips, pieces)),
            dma((chips, pieces)),
            dma((parts, 3)),
            dma((parts, 3)),
        ],
        compiler_params=pltpu.CompilerParams(
            collective_id=0, has_side_effects=True, vmem_limit_bytes=60 << 20
        ),
        name="gather_nodes",
    )(feats, norm, weight, bias, cot)


def scatter_kernel(
    nodes, parts, scale,
    partial_ref, norm_ref, sums_ref, hidden_ref,
    out_ref, sums_out, hidden_out,
    own_buf, sibling_buf, stage, arrived, small_part, small_stage, small_node,
    pass_send, pass_recv, send_sem, recv_sem, ps_send, ps_recv, ns_send, ns_recv,
    hid_send, hid_recv, own_sem,
):
    node, part = lax.axis_index("nodes"), lax.axis_index("feat")
    chips = nodes // 2
    chip, core = node // 2, node % 2
    rows = partial_ref.shape[2]
    other = chip * 2 + 1 - core
    chip_at = lambda d: (chip + d) % chips
    node_at = lambda d: {"nodes": chip_at(d) * 2 + core}
    square = chips == 4
    over_x = chip + 1 - 2 * (chip % 2)
    over_y = (chip + 2) % 4
    across = over_y + 1 - 2 * (chip % 2)
    node_of = lambda q: {"nodes": q * 2 + core}
    chip_of = (lambda d: (chip, over_x, over_y, across)[d]) if square else chip_at
    any_node = lambda d: {"nodes": (node + d) % nodes}
    part_at = lambda d: {"feat": (part + d) % parts}
    greet([any_node(d) for d in range(1, nodes)] + [part_at(d) for d in range(1, parts)])

    part_copies = []
    for d in range(1, parts):
        copy = remote(
            sums_ref.at[(part + d) % parts], small_part.at[d], ps_send.at[d], ps_recv.at[d], part_at(d)
        )
        copy.start()
        part_copies.append(copy)
    order = list(range(chips - 1, -1, -1))
    loads = {}
    passes = {}
    for d in order:
        copy = remote(
            partial_ref.at[chip_of(d) * 2 + 1 - core],
            sibling_buf.at[d],
            pass_send.at[d],
            pass_recv.at[d],
            {"nodes": other},
        )
        copy.start()
        passes[d] = copy
        load = pltpu.make_async_copy(
            partial_ref.at[chip_of(d) * 2 + core], own_buf.at[d], own_sem.at[d]
        )
        load.start()
        loads[d] = load
    quarter = rows // parts
    mine_cut = pl.ds(pl.multiple_of(part * quarter, quarter), quarter)
    hidden_copies = []
    for d in range(1, parts):
        copy = remote(
            hidden_ref.at[(part + d) % parts],
            hidden_out.at[:, mine_cut],
            hid_send.at[d],
            hid_recv.at[d],
            part_at(d),
        )
        copy.start()
        hidden_copies.append(copy)
    own_hidden = pltpu.make_async_copy(hidden_ref.at[part], hidden_out.at[:, mine_cut], own_sem.at[chips])
    own_hidden.start()

    directs = []

    def send(i, src, place, target):
        copy = remote(src, place, send_sem.at[i], recv_sem.at[i], node_of(target))
        copy.start()
        directs.append(copy)
        return copy

    def each(start, length, body):
        size = min(length, 1024)

        @pl.loop(0, length // size)
        def _(i):
            body(pl.ds(pl.multiple_of(start + i * size, size), size))

    half = rows // 2
    low, high = pl.ds(0, half), pl.ds(half, half)
    first = {}
    for d in order:
        loads[d].wait()
        passes[d].wait_recv()

        def join(cut, d=d):
            total = own_buf[d, :, cut].astype(jnp.float32) + sibling_buf[d, :, cut].astype(jnp.float32)
            if d == 0:
                out_ref[:, cut] = total
            else:
                stage[d, :, cut] = total.astype(stage.dtype)

        each(0, rows, join)
        if square:
            if d == 3:
                first["low"] = send(0, stage.at[3, :, low], arrived.at[1, :, low], over_y)
                first["high"] = send(1, stage.at[3, :, high], arrived.at[2, :, high], over_x)
            elif d == 2:
                send(2, stage.at[2, :, low], arrived.at[0, :, low], over_y)
            elif d == 1:
                send(3, stage.at[1, :, high], arrived.at[0, :, high], over_x)
        elif d:
            send(d, stage.at[d], arrived.at[d], chip_at(d))

    for copy in part_copies:
        copy.wait_recv()
    small_stage[...] = sums_ref[part]
    for d in range(1, parts):
        small_stage[...] += small_part[d]
    node_copies = []
    for d in range(1, nodes):
        copy = remote(small_stage, small_node.at[node], ns_send.at[d], ns_recv.at[d], any_node(d))
        copy.start()
        node_copies.append(copy)

    held = list(directs)
    if square:

        def add_stage(d):
            def body(cut):
                total = stage[d, :, cut].astype(jnp.float32) + arrived[d, :, cut].astype(jnp.float32)
                stage[d, :, cut] = total.astype(stage.dtype)

            return body

        first["low"].wait_recv()
        each(0, half, add_stage(1))
        send(4, stage.at[1, :, low], arrived.at[3, :, low], over_x)
        first["high"].wait_recv()
        each(half, half, add_stage(2))
        send(5, stage.at[2, :, high], arrived.at[3, :, high], over_y)
        held = directs[2:]
    for copy in node_copies:
        copy.wait_recv()
    small_node[node] = small_stage[...]
    total = small_node[0]
    for d in range(1, nodes):
        total = total + small_node[d]
    sums_out[...] = total * scale
    for copy in held:
        copy.wait_recv()

    def finish(cut):
        total = out_ref[:, cut]
        for d in (0, 3) if square else range(1, chips):
            total = total + arrived[d, :, cut].astype(jnp.float32)
        out_ref[:, cut] = norm_ref[:, cut] * total

    each(0, rows, finish)
    own_hidden.wait()
    for copy in hidden_copies:
        copy.wait()
    for copy in part_copies + node_copies + list(passes.values()) + directs:
        copy.wait_send()


def scatter_nodes(partial, norm, sums, hidden, parts, scale):
    nodes, feat, rows = partial.shape
    dma = pltpu.SemaphoreType.DMA
    chips = nodes // 2
    vmem = pl.BlockSpec(memory_space=pltpu.VMEM)
    big = pltpu.VMEM((chips, feat, rows), jnp.bfloat16)
    small = sums.shape[1:]
    return pl.pallas_call(
        functools.partial(scatter_kernel, nodes, parts, scale),
        out_shape=(
            jax.ShapeDtypeStruct((feat, rows), jnp.float32),
            jax.ShapeDtypeStruct(small, jnp.float32),
            jax.ShapeDtypeStruct((hidden.shape[1], rows), hidden.dtype),
        ),
        in_specs=[pl.BlockSpec(memory_space=pl.ANY)] + [vmem] * 3,
        out_specs=(vmem, vmem, vmem),
        scratch_shapes=[
            big, big, big, big,
            pltpu.VMEM((parts,) + small, jnp.float32),
            pltpu.VMEM(small, jnp.float32),
            pltpu.VMEM((nodes,) + small, jnp.float32),
            dma((chips,)), dma((chips,)), dma((max(chips, 6),)), dma((max(chips, 6),)),
            dma((parts,)), dma((parts,)), dma((nodes,)), dma((nodes,)),
            dma((parts,)), dma((parts,)), dma((chips + 1,)),
        ],
        compiler_params=pltpu.CompilerParams(
            collective_id=1, has_side_effects=True, vmem_limit_bytes=60 << 20
        ),
        name="scatter_nodes",
    )(partial, norm, sums, hidden)


def middle_kernel(
    parts, pieces,
    agg_ref, weight_ref, bias_ref, cot_ref, norm_ref,
    back_out, hidden_out, sums_out,
    agg, grad_pre, stage, in_send, in_recv, out_send, out_recv,
):
    part = lax.axis_index("feat")
    _, feat, quarter = agg.shape
    width = quarter // pieces
    hid_local = cot_ref.shape[1]
    hid = parts * hid_local
    part_at = lambda d: {"feat": (part + d) % parts}
    at = lambda d, k: pl.ds(
        pl.multiple_of((part + d) % parts * quarter + k * width, width), width
    )
    cuts = [pl.ds(k * width, width) for k in range(pieces)]
    greet([part_at(d) for d in range(1, parts)])

    arriving = {}
    for k, cut in enumerate(cuts):
        for d in range(1, parts):
            copy = remote(
                agg_ref.at[:, at(d, k)], agg.at[part, :, cut], in_send.at[d, k], in_recv.at[d, k], part_at(d)
            )
            copy.start()
            arriving[d, k] = copy
    for k, cut in enumerate(cuts):
        agg[part, :, cut] = agg_ref[:, at(0, k)]

    leaving = []
    for k, cut in enumerate(cuts):
        for d in range(1, parts):
            arriving[d, k].wait_recv()
        columns = agg[:, :, cut].reshape(parts * feat, width)
        pre = (
            lax.dot_general(
                weight_ref[...], columns, (((0,), (0,)), ((), ())), preferred_element_type=jnp.float32
            )
            + bias_ref[:, :1]
        )
        sigma = jax.nn.sigmoid(pre)
        hidden_out[:, :, cut] = (pre * sigma).astype(jnp.bfloat16).reshape(parts, hid_local, width)
        cot = cot_ref[:, :, cut].reshape(hid, width).astype(jnp.float32)
        grad = (cot * (sigma * (1.0 + pre * (1.0 - sigma)))).astype(jnp.bfloat16)
        grad_pre[:, cut] = grad
        back = norm_ref[:, at(0, k)] * lax.dot_general(
            weight_ref[...], grad, NN, preferred_element_type=jnp.float32
        )
        stage[:, :, cut] = back.astype(jnp.bfloat16).reshape(parts, feat, width)
        for d in range(1, parts):
            copy = remote(
                stage.at[(part + d) % parts, :, cut], back_out.at[:, at(0, k)],
                out_send.at[d, k], out_recv.at[d, k], part_at(d),
            )
            copy.start()
            leaving.append(copy)
        back_out[:, at(0, k)] = stage[part, :, cut]

    grads = grad_pre[...]
    sums_out[:, :feat] = lax.dot_general(
        agg[...].reshape(parts * feat, quarter), grads, NT, preferred_element_type=jnp.float32
    ).reshape(parts, feat, hid)
    bias_rows = lax.dot_general(
        jnp.ones((8, quarter), jnp.bfloat16), grads, NT, preferred_element_type=jnp.float32
    )
    for d in range(parts):
        sums_out[d, feat:] = bias_rows
    for copy in arriving.values():
        copy.wait_send()
    for copy in leaving:
        copy.wait()


def middle(aggregated, weight, bias, cot, norm, pieces=8):
    feat, rows = aggregated.shape
    parts, hid_local, quarter = cot.shape
    hid = parts * hid_local
    dma = pltpu.SemaphoreType.DMA((parts, pieces))
    vmem = pl.BlockSpec(memory_space=pltpu.VMEM)
    return pl.pallas_call(
        functools.partial(middle_kernel, parts, pieces),
        out_shape=(
            jax.ShapeDtypeStruct((feat, rows), jnp.bfloat16),
            jax.ShapeDtypeStruct(cot.shape, jnp.bfloat16),
            jax.ShapeDtypeStruct((parts, feat + 8, hid), jnp.float32),
        ),
        in_specs=[vmem] * 5,
        out_specs=(vmem, vmem, vmem),
        scratch_shapes=[
            pltpu.VMEM((parts, feat, quarter), jnp.bfloat16),
            pltpu.VMEM((hid, quarter), jnp.bfloat16),
            pltpu.VMEM((parts, feat, quarter), jnp.bfloat16),
            dma, dma, dma, dma,
        ],
        compiler_params=pltpu.CompilerParams(
            collective_id=2, has_side_effects=True, vmem_limit_bytes=60 << 20
        ),
        name="middle",
    )(aggregated, weight, bias, cot, norm)


def on_device(feats, tiles, dst_block, src_block, tile_counts, norm, weight, bias, cotangent):
    rows, feat_local = feats.shape
    hid_local = cotangent.shape[1]
    nodes, parts = lax.axis_size("nodes"), lax.axis_size("feat")
    norm_row = norm[None, :]
    counts, src, dst = tile_counts, src_block[0], dst_block[0]
    bias_columns = jnp.broadcast_to(bias[:, None], (hid_local, 128))
    shards, full_weight, full_bias, cot = gather_nodes(
        feats.T, norm_row, weight, bias_columns, cotangent.T, nodes, parts
    )
    full_weight = full_weight.reshape(parts * feat_local, -1)
    full_bias = full_bias.reshape(parts * hid_local, 128)
    aggregated = forward_tiles(counts, src, dst, tiles, shards, norm_row)
    back, hidden, sums = middle(aggregated, full_weight, full_bias, cot, norm_row)
    partial = backward_tiles(counts, src, dst, tiles, back)
    scale = (rows * nodes) ** (-0.5)
    grad_feats, sums, hidden = scatter_nodes(partial, norm_row, sums, hidden, parts, scale)
    grad_weight = sums[:feat_local]
    grad_bias = lax.dynamic_slice_in_dim(
        sums[feat_local], lax.axis_index("feat") * hid_local, hid_local, 0
    )
    return (hidden.T, grad_weight, grad_bias, grad_feats.T)


def solution(mesh):
    return jax.shard_map(
        on_device,
        mesh=mesh,
        in_specs=(
            P("nodes", "feat"),
            P("nodes", None, None, None, None),
            P("nodes", None, None),
            P("nodes", None, None),
            P("nodes", None),
            P("nodes"),
            P("feat", None),
            P("feat"),
            P("nodes", "feat"),
        ),
        out_specs=(P("nodes", "feat"), P("feat", None), P("feat"), P("nodes", "feat")),
        check_vma=False,
    )
```
